32 devices in a mesh: tm: 8 (over z, y), fsdp: 4 (over x, core).
Axes of the slice: x: 2, y: 2, z: 4, core: 2. Of those that a mesh axis runs over, the one named last changes fastest.
Arguments:
- inputs: bfloat16 [4, 2048, 2048], P('fsdp', 'tm'), may hold values from -6 to 6
- query_rows: bfloat16 [4, 2048, 1024], P('fsdp', 'tm'), may hold values from -8 to 8
- saved_key_rows: bfloat16 [4, 2048, 1024], P('fsdp', 'tm'), may hold values from -8 to 8
- value_rows: bfloat16 [4, 2048, 1024], P('fsdp', 'tm'), may hold values from -6 to 6
- grad_out: bfloat16 [4, 2048, 1024], P('fsdp', 'tm'), may hold values from -24 to 24
- key_weight: bfloat16 [2048, 1024], P('fsdp'), may hold values from -0.125 to 0.125
- value_weight: bfloat16 [2048, 1024], P('fsdp'), may hold values from -0.125 to 0.125
- block_pairs: int32 [8, 8, 2], P('tm'), may hold values from 0 to 15, as said below
- pair_counts: int32 [8], P('tm'), may hold values from 2 to 8, as said below
Outputs:
- grad_query: bfloat16 [4, 2048, 1024], P('fsdp', 'tm')
- input_gradient_rows: bfloat16 [4, 2048, 2048], P('fsdp', 'tm')
- grad_key_weight: float32 [2048, 1024], P('fsdp', 'tm')
- grad_value_weight: float32 [2048, 1024], P('fsdp', 'tm')
The draws below stay inside these ranges and needn't reach their ends.
Inputs may be any that keep to these rules, and one draw needn't show every extreme that they name: `block_pairs`: row r of shard j names (query block, key block) by block numbers along the sequence. The first pair_counts[j] rows are shard j's part of the mask: the query block is one of shard j's 2 blocks, the key block is at most the query block and above the query block minus 4, no pair stands twice, and each of the shard's query blocks is paired with itself. Rows from pair_counts[j] on are not part of the mask. `pair_counts`: some shard holds all 8 pairs of its band in every draw.
All inputs are finite; a program needn't handle non-finite values.
Results may differ from the reference program's by a relative error of at most 0.012.
Values may be sent and summed in bfloat16 or wider, within the bound.
No kernel may reach another device: no remote copies, remote signals or barrier semaphores. Data moves between devices by JAX's collectives and lax.ppermute only.
A program may use at most 128 MiB of HBM per device.

```python
import jax
import jax.numpy as jnp
from jax import lax

D = 2048
H = 8
HS = 128
BLK = 128
WB = 4
TOK_DEV = 256
HD = 1024
QBD = 2
REACH = 2
MAXP = 8
L = 2048
SEQS = 4
N_TM = 8


def draw_query_rows(key, part):
    values = jnp.clip(jax.random.normal(jax.random.fold_in(key, 3), (SEQS, L, HD), jnp.float32), -6.0, 6.0)
    return values.astype(jnp.bfloat16)


def draw_saved_key_rows(key, part):
    values = jnp.clip(jax.random.normal(jax.random.fold_in(key, 5), (SEQS, L, HD), jnp.float32), -6.0, 6.0)
    return values.astype(jnp.bfloat16)


def mask_tables(key):
    base = jax.random.fold_in(key, 29)
    shard_ids = jnp.arange(N_TM)[:, None]
    slot_ids = jnp.arange(MAXP)[None, :]
    query_block = shard_ids * QBD + slot_ids // WB
    key_block = query_block - slot_ids % WB
    row_boundaries = jax.random.randint(jax.random.fold_in(base, 1), (N_TM, 1), 10, 101)
    dense_shard = jax.random.randint(jax.random.fold_in(base, 2), (), REACH, N_TM)
    row_boundaries = jnp.where(shard_ids == dense_shard, 101, row_boundaries)
    rolls = jax.random.randint(jax.random.fold_in(base, 3), (N_TM, MAXP), 0, 100)
    kept = (slot_ids % WB == 0) | (key_block >= 0) & (rolls < row_boundaries)
    ranking = jnp.where(kept, 0, MAXP) + slot_ids
    ordering = jnp.argsort(ranking, axis=1)
    listed = jnp.stack((query_block, jnp.maximum(key_block, 0)), axis=2)
    listed = jnp.take_along_axis(listed, ordering[:, :, None], axis=1)
    totals = jnp.sum(kept.astype(jnp.int32), axis=1)
    return (listed.astype(jnp.int32), totals.astype(jnp.int32))


def draw_block_pairs(key, part):
    listed, totals = mask_tables(key)
    return listed


def draw_pair_counts(key, part):
    listed, totals = mask_tables(key)
    return totals


def steps_of(stream_key, dims, pieces, low, high):
    def one(axis_at, shards_of):
        steps = jax.random.uniform(jax.random.fold_in(jax.random.fold_in(stream_key, 6), axis_at), (shards_of,), jnp.float32, low / len(pieces), high / len(pieces))
        return jnp.repeat(jnp.exp(steps), dims[axis_at] // shards_of).reshape((-1,) + (1,) * (len(dims) - axis_at - 1))

    loudness = one(*pieces[0])
    for cut in pieces[1:]:
        loudness = loudness * one(*cut)
    return loudness


def bell_draw(key, shape, deviation, most, split=(), kind=jnp.bfloat16):
    entries = deviation * jax.random.normal(key, shape, jnp.float32)
    if split:
        entries = entries * steps_of(key, shape, split, -0.22, 0.18)
    return jnp.clip(entries, -most, most).astype(kind)


def setup_inputs(seed: int = 0) -> dict:
    keys = jax.random.split(jax.random.key(seed), 10)
    inputs = bell_draw(keys[0], (SEQS, L, D), 1.0, 6.0, ((0, 4), (1, 8)))
    query_rows = draw_query_rows(jax.random.fold_in(keys[9], 71), 0)
    saved_key_rows = draw_saved_key_rows(jax.random.fold_in(keys[9], 71), 0)
    value_rows = bell_draw(keys[3], (SEQS, L, HD), 1.0, 6.0, ((0, 4), (1, 8)))
    grad_out = bell_draw(keys[4], (SEQS, L, HD), 4.0, 24.0, ((0, 4), (1, 8)))
    key_weight = bell_draw(keys[5], (D, HD), D ** -0.5, 0.125, ((0, 4),))
    value_weight = bell_draw(keys[6], (D, HD), D ** -0.5, 0.125, ((0, 4),))
    block_pairs = draw_block_pairs(jax.random.fold_in(keys[9], 71), 0)
    pair_counts = draw_pair_counts(jax.random.fold_in(keys[9], 71), 0)
    return {"inputs": inputs, "query_rows": query_rows, "saved_key_rows": saved_key_rows, "value_rows": value_rows, "grad_out": grad_out, "key_weight": key_weight, "value_weight": value_weight, "block_pairs": block_pairs, "pair_counts": pair_counts}


def head_terms(allowed, query_head, key_head, value_head, cotangent_head):
    score_scale = query_head.shape[-1] ** -0.5
    query_wide = query_head.astype(jnp.float32)
    key_wide = key_head.astype(jnp.float32)
    value_wide = value_head.astype(jnp.float32)
    cotangent_wide = cotangent_head.astype(jnp.float32)
    scores = jnp.einsum("qd,kd->qk", query_wide, key_wide) * score_scale
    scores = jnp.where(allowed, scores, -jnp.inf)
    largest = jnp.max(scores, axis=1, keepdims=True)
    weights = jnp.exp(scores - largest)
    weights = weights / jnp.sum(weights, axis=1, keepdims=True)
    weights_low = weights.astype(jnp.bfloat16)
    weights_back = weights_low.astype(jnp.float32)
    attended = jnp.einsum("qk,kd->qd", weights_back, value_wide)
    row_dot = jnp.sum(cotangent_wide * attended, axis=1, keepdims=True)
    grad_probs = jnp.einsum("qd,kd->qk", cotangent_wide, value_wide)
    grad_low = (weights * (grad_probs - row_dot)).astype(jnp.bfloat16)
    grad_back = grad_low.astype(jnp.float32)
    grad_q = jnp.einsum("qk,kd->qd", grad_back, key_wide) * score_scale
    grad_k = jnp.einsum("qk,qd->kd", grad_back, query_wide) * score_scale
    grad_v = jnp.einsum("qk,qd->kd", weights_back, cotangent_wide)
    return grad_q, grad_k, grad_v


def split_heads(array):
    return jnp.transpose(array.reshape(array.shape[0], H, HS), (1, 0, 2))


def join_heads(array):
    return jnp.transpose(array, (1, 0, 2)).reshape(array.shape[1], H * HS)


def reference(inputs, query_rows, saved_key_rows, value_rows, grad_out, key_weight, value_weight, block_pairs, pair_counts):
    window_len = (REACH + 1) * TOK_DEV
    nblocks = L // BLK
    is_valid = (jnp.arange(MAXP)[None, :] < pair_counts[:, None]).astype(jnp.int32)
    block_table = jnp.zeros((nblocks, nblocks), jnp.int32)
    block_table = block_table.at[block_pairs[:, :, 0].reshape(-1), block_pairs[:, :, 1].reshape(-1)].max(is_valid.reshape(-1))
    block_table = jnp.concatenate((jnp.zeros((nblocks, REACH * QBD), jnp.int32), block_table), axis=1)

    def sequence_grads(operands):
        query_seq, key_seq, value_seq, cotangent_seq = operands
        front = jnp.zeros((REACH * TOK_DEV, HD), key_seq.dtype)
        key_pad = jnp.concatenate((front, key_seq), axis=0)
        value_pad = jnp.concatenate((front, value_seq), axis=0)

        def shard_grads(shard_id):
            row_start = shard_id * TOK_DEV
            query_portion = lax.dynamic_slice_in_dim(query_seq, row_start, TOK_DEV, 0)
            cotangent_part = lax.dynamic_slice_in_dim(cotangent_seq, row_start, TOK_DEV, 0)
            key_window = lax.dynamic_slice_in_dim(key_pad, row_start, window_len, 0)
            value_window = lax.dynamic_slice_in_dim(value_pad, row_start, window_len, 0)
            block_allowed = lax.dynamic_slice(block_table, (shard_id * QBD, shard_id * QBD), (QBD, (REACH + 1) * QBD)) > 0
            tile_allowed = jnp.repeat(jnp.repeat(block_allowed, BLK, axis=0), BLK, axis=1)
            query_pos = row_start + jnp.arange(TOK_DEV, dtype=jnp.int32)
            key_pos = row_start - REACH * TOK_DEV + jnp.arange(window_len, dtype=jnp.int32)
            allowed = tile_allowed & (key_pos[None, :] <= query_pos[:, None])

            def per_head(head_ops):
                return head_terms(allowed, head_ops[0], head_ops[1], head_ops[2], head_ops[3])

            head_q, head_k, head_v = lax.map(per_head, (split_heads(query_portion), split_heads(key_window), split_heads(value_window), split_heads(cotangent_part)))
            return join_heads(head_q).astype(jnp.bfloat16), join_heads(head_k), join_heads(head_v)

        shard_q, shard_k, shard_v = lax.map(shard_grads, jnp.arange(N_TM, dtype=jnp.int32))
        grad_keys = shard_k[:, REACH * TOK_DEV:, :]
        grad_values = shard_v[:, REACH * TOK_DEV:, :]
        for offset in range(1, REACH + 1):
            lowest_row_index = (REACH - offset) * TOK_DEV
            padding_values = jnp.zeros((offset, TOK_DEV, HD), jnp.float32)
            piece_k = shard_k[:, lowest_row_index:lowest_row_index + TOK_DEV, :]
            piece_v = shard_v[:, lowest_row_index:lowest_row_index + TOK_DEV, :]
            grad_keys = grad_keys + jnp.concatenate((piece_k[offset:], padding_values), axis=0)
            grad_values = grad_values + jnp.concatenate((piece_v[offset:], padding_values), axis=0)
        return shard_q.reshape(L, HD), grad_keys.reshape(L, HD), grad_values.reshape(L, HD)

    grad_query, grad_keys, grad_values = lax.map(sequence_grads, (query_rows, saved_key_rows, value_rows, grad_out))
    paired_lower_rows = jnp.concatenate((grad_keys.astype(jnp.bfloat16), grad_values.astype(jnp.bfloat16)), axis=2)
    paired_weight_matrices = jnp.concatenate((key_weight, value_weight), axis=1).astype(jnp.float32)
    input_gradient_rows = jnp.einsum("ixn,kn->ixk", paired_lower_rows.astype(jnp.float32), paired_weight_matrices).astype(jnp.bfloat16)
    shaped_inputs = jnp.transpose(inputs.reshape(SEQS, N_TM, TOK_DEV, D), (1, 0, 2, 3))
    shaped_grads = jnp.transpose(paired_lower_rows.reshape(SEQS, N_TM, TOK_DEV, 2 * HD), (1, 0, 2, 3))

    def shard_weights(total, operands):
        input_shard, grad_shard = operands
        partials = jnp.einsum("std,stc->sdc", input_shard.astype(jnp.float32), grad_shard.astype(jnp.float32))
        return total + jnp.sum(partials, axis=0), None

    weight_grads, unused = lax.scan(shard_weights, jnp.zeros((D, 2 * HD), jnp.float32), (shaped_inputs, shaped_grads))
    return (grad_query, input_gradient_rows, weight_grads[:, :HD], weight_grads[:, HD:])
```

```python
import functools

import jax
import jax.numpy as jnp
from jax import lax
from jax.experimental import pallas as pl
from jax.experimental.pallas import tpu as pltpu
from jax.sharding import PartitionSpec as P

H = 8
HS = 128
BLK = 128
HD = 1024
QBD = 2
REACH = 2
MAXP = 8
SLOTS = QBD + 3
SPAN = SLOTS * BLK
LOWEST = -1e29
MASKED = -1e30
SCALE = HS ** (-0.5)
GROUPS = ((0, 1, 2, 3, 4, 5, 6, 7),)
VMEM = pl.BlockSpec(memory_space=pltpu.VMEM)
SMEM = pl.BlockSpec(memory_space=pltpu.SMEM)


def kernel_call(body, outs, operands, scalars=0, scratch=(), flops=0):
    moved = sum(x.size * x.dtype.itemsize for x in (*operands, *outs))
    return pl.pallas_call(
        body,
        out_shape=tuple(outs),
        in_specs=[SMEM] * scalars + [VMEM] * (len(operands) - scalars),
        out_specs=tuple([VMEM] * len(outs)),
        scratch_shapes=list(scratch),
        compiler_params=pltpu.CompilerParams(vmem_limit_bytes=40 * 1024 * 1024),
        cost_estimate=pl.CostEstimate(flops=flops, bytes_accessed=moved, transcendentals=0),
    )(*operands)


def shape(dims, kind):
    return jax.ShapeDtypeStruct(dims, kind)


def shifted(value, axis, steps):
    count = lax.axis_size(axis)
    return lax.ppermute(
        value, axis, [(s, s + steps) for s in range(max(0, -steps), min(count, count - steps))]
    )


def rolled_pairs(count, far, flip):
    half = count // 2
    return [(((a + far) % half) * 2 + (b ^ flip), a * 2 + b) for a in range(half) for b in range(2)]


def nt(left, right):
    return lax.dot_general(left, right, (((1,), (1,)), ((), ())), preferred_element_type=jnp.float32)


def tn(left, right):
    return lax.dot_general(left, right, (((0,), (0,)), ((), ())), preferred_element_type=jnp.float32)


def nn(left, right):
    return jnp.dot(left, right, preferred_element_type=jnp.float32)


def fill_bias(tables, bias):
    rows = lax.broadcasted_iota(jnp.int32, (BLK, BLK), 0)
    columns = lax.broadcasted_iota(jnp.int32, (BLK, BLK), 1)
    for key in range(QBD):
        for slot in range(SLOTS):
            place = (pl.ds(key * BLK, BLK), pl.ds(slot * BLK, BLK))
            if not 0 <= slot - key <= 3:
                bias[place] = jnp.full((BLK, BLK), MASKED, jnp.float32)
                continue
            step = slot // QBD
            table = tables[step]
            hit = jnp.int32(0)
            for row in range(MAXP):
                same = (table[2 * row] == slot - QBD * step) & (table[2 * row + 1] == key - QBD * step)
                hit = hit + jnp.where(same & (row < table[2 * MAXP]), 1, 0)
            value = jnp.where(hit > 0, 0.0, MASKED).astype(jnp.float32)
            block = jnp.full((BLK, BLK), value, jnp.float32)
            if slot == key:
                block = jnp.where(rows <= columns, block, MASKED)
            bias[place] = block


def head_of(ref, place):
    return ref[:, place * HS : (place + 1) * HS]


def queries_of(own, near, far, head, place):
    return jnp.concatenate([head_of(own, head), head_of(near, place), head_of(far, place)], axis=0)


def stats_body(heads, t0, t1, t2, q, k, v, g, near, far, own, up1, up2, down1, down2, bias):
    count = len(heads)
    fill_bias((t0, t1, t2), bias)
    for n, h in enumerate(heads):
        query = queries_of(q, near, far, h, n)
        cotangent = queries_of(g, near, far, h, count + n)
        scores = nt(head_of(k, h), query) * SCALE + bias[...]
        products = nt(head_of(v, h), cotangent)
        largest = jnp.maximum(jnp.max(scores, axis=0, keepdims=True), LOWEST)
        weights = jnp.exp(scores - largest)
        own[n : n + 1, :] = largest
        own[count + n : count + n + 1, :] = jnp.sum(weights, axis=0, keepdims=True)
        own[2 * count + n : 2 * count + n + 1, :] = jnp.sum(weights * products, axis=0, keepdims=True)
    up1[...] = own[:, 2 * BLK :]
    up2[...] = own[:, 4 * BLK :]
    down1[...] = own[:, : 3 * BLK]
    down2[...] = own[:, :BLK]


def grads_body(
    heads, t0, t1, t2, q, k, v, g, near, far, own, from1, from2, back1, back2,
    low, dq0, dq1, dq2, bias, total,
):
    count = len(heads)
    fill_bias((t0, t1, t2), bias)

    def terms(ref, first, last):
        part = ref[:, first * BLK : last * BLK]
        large, mass, dot = (part[i * count : (i + 1) * count] for i in range(3))
        return jnp.where(mass > 0, large, LOWEST), mass, dot

    nothing = (
        jnp.full((count, BLK), LOWEST, jnp.float32),
        jnp.zeros((count, BLK), jnp.float32),
        jnp.zeros((count, BLK), jnp.float32),
    )

    def side(*parts):
        return tuple(jnp.concatenate(piece, axis=1) for piece in zip(*parts))

    sets = (
        terms(own, 0, SLOTS),
        side(terms(from1, 0, 3), terms(back1, 1, 3)),
        side(terms(from2, 0, 1), nothing, terms(back1, 0, 1), nothing, terms(back2, 0, 1)),
    )
    largest = jnp.maximum(jnp.maximum(sets[0][0], sets[1][0]), sets[2][0])
    mass = jnp.zeros((count, SPAN), jnp.float32)
    dot = jnp.zeros((count, SPAN), jnp.float32)
    for large, part_mass, part_dot in sets:
        factor = jnp.exp(large - largest)
        mass = mass + factor * part_mass
        dot = dot + factor * part_dot
    inverse = jnp.where(mass > 0, 1.0 / jnp.where(mass > 0, mass, 1.0), 0.0)
    total[0, :count] = largest
    total[1, :count] = inverse
    total[2, :count] = dot * inverse
    for n, h in enumerate(heads):
        query = queries_of(q, near, far, h, n)
        cotangent = queries_of(g, near, far, h, count + n)
        key = head_of(k, h)
        scores = nt(key, query) * SCALE + bias[...]
        products = nt(head_of(v, h), cotangent)
        probs = jnp.exp(scores - total[0, n : n + 1, :]) * total[1, n : n + 1, :]
        grad_scores = (probs * (products - total[2, n : n + 1, :])).astype(jnp.bfloat16)
        columns = slice(n * HS, (n + 1) * HS)
        low[:, columns] = (nn(grad_scores, query) * SCALE).astype(jnp.bfloat16)
        low[:, (count + n) * HS : (count + n + 1) * HS] = nn(
            probs.astype(jnp.bfloat16), cotangent
        ).astype(jnp.bfloat16)
        grad_query = tn(grad_scores, key) * SCALE
        dq0[:, columns] = grad_query[: 2 * BLK]
        dq1[:, columns] = grad_query[2 * BLK : 4 * BLK].astype(jnp.bfloat16)
        dq2[:, columns] = grad_query[4 * BLK :].astype(jnp.bfloat16)


def weight_body(pairs, parts, count, y_ref, turned, *refs):
    lows, (send, keep) = refs[:parts], refs[parts:]
    tokens = lows[0].shape[0]
    mine = y_ref[0]
    for out, side in ((send, 1 - mine), (keep, mine)):
        for pair in range(pairs):
            first = pl.multiple_of((2 * pair + side) * HS, HS)
            second = pl.multiple_of((count + 2 * pair + side) * HS, HS)
            total = None
            for part, low in enumerate(lows):
                right = jnp.concatenate([low[:, pl.ds(first, HS)], low[:, pl.ds(second, HS)]], axis=1)
                term = nn(turned[:, part * tokens : (part + 1) * tokens], right)
                total = term if total is None else total + term
            out[:, pair * 2 * HS : (pair + 1) * 2 * HS] = total.astype(out.dtype)


def plain_weight_body(parts, turned, *refs):
    lows, out = refs[:parts], refs[parts]
    tokens = lows[0].shape[0]
    for first in range(0, lows[0].shape[1], 2 * HS):
        total = None
        for part, low in enumerate(lows):
            term = nn(turned[:, part * tokens : (part + 1) * tokens], low[:, first : first + 2 * HS])
            total = term if total is None else total + term
        out[:, first : first + 2 * HS] = total


def rows_body(heads, parts, has_base, *refs):
    lows, key_weight, value_weight = refs[:parts], refs[parts], refs[parts + 1]
    bases = refs[parts + 2 : 2 * parts + 2] if has_base else ()
    outs = refs[-parts:]
    width = len(heads) * HS
    if width == HD:
        weights = (key_weight[...], value_weight[...])
    else:
        weights = tuple(
            jnp.concatenate([head_of(w, h) for h in heads], axis=1) for w in (key_weight, value_weight)
        )
    for part, low in enumerate(lows):
        total = nt(low[:, :width], weights[0]) + nt(low[:, width:], weights[1])
        if has_base:
            total = total + bases[part][...]
        outs[part][...] = total.astype(outs[part].dtype)


def chunks_body(places, place_ref, keep, heard, *outs):
    width = 2 * HS
    for index in range(places):
        columns = pl.ds(pl.multiple_of(place_ref[index] * width, width), width)
        value = keep[:, columns] + heard[:, columns].astype(jnp.float32)
        outs[index][...] = value.astype(outs[index].dtype)


def shards(
    inputs, query_rows, saved_key_rows, value_rows, grad_out, key_weight, value_weight, block_pairs, pair_counts
):
    tokens = query_rows.shape[1]
    n_tm, n_fsdp = lax.axis_size("tm"), lax.axis_size("fsdp")
    shard, owner = lax.axis_index("tm"), lax.axis_index("fsdp")
    d_model = inputs.shape[2]
    rows = d_model // n_fsdp
    q, k, v, g = query_rows[0], saved_key_rows[0], value_rows[0], grad_out[0]
    bf16, f32 = jnp.bfloat16, jnp.float32

    def columns_of(array, heads):
        return [array[:, h * HS : (h + 1) * HS] for h in heads] if len(heads) < H else [array]

    halos = []
    for heads in GROUPS:
        packed = jnp.concatenate(columns_of(q, heads) + columns_of(g, heads), axis=1)
        halos.append((shifted(packed, "tm", -1), shifted(packed[:BLK], "tm", -2)))
    table = jnp.concatenate([(block_pairs[0] - shard * QBD).reshape(-1), pair_counts])
    tables = (table, shifted(table, "tm", -1), shifted(table, "tm", -2))

    relative = [(far, flip) for far in range(n_fsdp // 2) for flip in range(2)]
    pieces = []
    for far, flip in relative:
        target = ((owner // 2 - far) % (n_fsdp // 2)) * 2 + (owner % 2 ^ flip)
        piece = lax.dynamic_slice_in_dim(inputs[0], target * rows, rows, 1)
        if far or flip:
            piece = lax.ppermute(piece, "fsdp", rolled_pairs(n_fsdp, far, flip))
        pieces.append(piece.T)
    turned = jnp.concatenate(pieces, axis=1)

    gathered, query_terms = [], []
    for heads, (near, far_rows) in zip(GROUPS, halos):
        count = len(heads)
        width = count * HS
        operands = (*tables, q, k, v, g, near, far_rows)
        height = -(-3 * count // 8) * 8
        own, up1, up2, down1, down2 = kernel_call(
            functools.partial(stats_body, heads),
            [shape((height, n * BLK), f32) for n in (SLOTS, 3, 1, 3, 1)],
            operands,
            scalars=3,
            scratch=[pltpu.VMEM((tokens, SPAN), f32)],
            flops=4 * tokens * SPAN * width,
        )
        stats = (
            own, shifted(up1, "tm", 1), shifted(up2, "tm", 2), shifted(down1, "tm", -1), shifted(down2, "tm", -2)
        )
        low, dq0, dq1, dq2 = kernel_call(
            functools.partial(grads_body, heads),
            [
                shape((tokens, 2 * width), bf16),
                shape((tokens, width), f32),
                shape((tokens, width), bf16),
                shape((BLK, width), bf16),
            ],
            (*operands, *stats),
            scalars=3,
            scratch=[pltpu.VMEM((tokens, SPAN), f32), pltpu.VMEM((3, 8, SPAN), f32)],
            flops=10 * tokens * SPAN * width,
        )
        lows = []
        for far in range(n_fsdp // 2):
            there = low if far == 0 else lax.ppermute(low, "fsdp", rolled_pairs(n_fsdp, far, 0))
            lows += [there, lax.ppermute(there, "fsdp", rolled_pairs(n_fsdp, 0, 1))]
        gathered.append(lows)
        query_terms.append((dq0, shifted(dq1, "tm", 1), shifted(dq2, "tm", 2)))

    column_width = HD // n_tm
    half = n_tm // 2
    key_total = value_total = None
    bases = None
    for index, (heads, lows) in enumerate(zip(GROUPS, gathered)):
        count = len(heads)
        parts = len(lows)
        work = 2 * rows * tokens * parts * 2 * count * HS
        if column_width == HS:
            pairs = count // 2
            send, keep = kernel_call(
                functools.partial(weight_body, pairs, parts, count),
                [shape((rows, count * HS), bf16), shape((rows, count * HS), f32)],
                (jnp.reshape(shard % 2, (1,)), turned, *lows),
                scalars=1,
                flops=work,
            )
            heard = lax.ppermute(send, "tm", rolled_pairs(n_tm, 0, 1))
            goal = [[heads[2 * n + y] // 2 for n in range(pairs)] for y in range(2)]
            routes, places = [], []
            for far in range(half):
                routes.append([(((z + far) % half) * 2 + y, z * 2 + y) for y in range(2) for z in goal[y]])
                lookup = [0] * n_tm
                for y in range(2):
                    for n, z in enumerate(goal[y]):
                        lookup[((z + far) % half) * 2 + y] = n
                places.append(jnp.asarray(lookup, jnp.int32)[shard])
            parcels = kernel_call(
                functools.partial(chunks_body, half),
                [shape((rows, 2 * HS), f32 if far == 0 else bf16) for far in range(half)],
                (jnp.stack(places), keep, heard),
                scalars=1,
            )
            total = parcels[0]
            for far in range(1, half):
                total = total + lax.ppermute(parcels[far], "tm", routes[far]).astype(f32)
            if key_total is None:
                key_total, value_total = total[:, :HS], total[:, HS:]
            else:
                mine = jnp.asarray([any(h == j for h in heads) for j in range(n_tm)])[shard]
                key_total = jnp.where(mine, total[:, :HS], key_total)
                value_total = jnp.where(mine, total[:, HS:], value_total)
        else:
            (partial,) = kernel_call(
                functools.partial(plain_weight_body, parts),
                [shape((rows, 2 * count * HS), f32)],
                (turned, *lows),
                flops=work,
            )
            bases_w = partial if index == 0 else jnp.concatenate([bases_w, partial], axis=1)
        last = index == len(GROUPS) - 1
        bases = kernel_call(
            functools.partial(rows_body, heads, parts, index > 0),
            [shape((tokens, rows), bf16 if last else f32)] * parts,
            (*lows, key_weight, value_weight, *(bases or ())),
            flops=work,
        )
    if column_width != HS:
        order = [h for heads in GROUPS for h in heads]
        starts = []
        for side in range(2):
            found = {}
            base = 0
            for heads in GROUPS:
                for n, h in enumerate(heads):
                    found[h] = base + (side * len(heads) + n) * HS
                base += 2 * len(heads) * HS
            starts.append(found)
        key_total, value_total = (
            lax.psum_scatter(
                jnp.concatenate([bases_w[:, found[h] : found[h] + HS] for h in sorted(order)], axis=1),
                "tm",
                scatter_dimension=1,
                tiled=True,
            )
            for found in starts
        )

    result = jnp.zeros((tokens, d_model), bf16)
    for (far, flip), piece in zip(relative, bases):
        if far or flip:
            routes = [(receiver, sender) for sender, receiver in rolled_pairs(n_fsdp, far, flip)]
            piece = lax.ppermute(piece, "fsdp", routes)
        source = ((owner // 2 - far) % (n_fsdp // 2)) * 2 + (owner % 2 ^ flip)
        result = lax.dynamic_update_slice_in_dim(result, piece, source * rows, 1)

    by_head = [None] * H
    for heads, (dq0, near, far_rows) in zip(GROUPS, query_terms):
        full = dq0 + near.astype(f32)
        full = jnp.concatenate([full[:BLK] + far_rows.astype(f32), full[BLK:]], axis=0).astype(bf16)
        for n, h in enumerate(heads):
            by_head[h] = full[:, n * HS : (n + 1) * HS] if len(heads) < H else full
    grad_query = by_head[0] if len(GROUPS) == 1 else jnp.concatenate(by_head, axis=1)
    return (grad_query[None], result[None], key_total, value_total)


def solution(mesh):
    return jax.shard_map(
        shards,
        mesh=mesh,
        in_specs=(
            P("fsdp", "tm", None),
            P("fsdp", "tm", None),
            P("fsdp", "tm", None),
            P("fsdp", "tm", None),
            P("fsdp", "tm", None),
            P("fsdp", None),
            P("fsdp", None),
            P("tm", None, None),
            P("tm"),
        ),
        out_specs=(P("fsdp", "tm", None), P("fsdp", "tm", None), P("fsdp", "tm"), P("fsdp", "tm")),
        check_vma=False,
    )
```

```python
import functools

import jax
import jax.numpy as jnp
from jax import lax
from jax.experimental import pallas as pl
from jax.experimental.pallas import tpu as pltpu
from jax.sharding import PartitionSpec as P

H = 8
HS = 128
BLK = 128
HD = 1024
QBD = 2
REACH = 2
MAXP = 8
WB = 4
SLOTS = QBD + WB - 1
RULES = 16
VMEM_LIMIT = 24 * 1024 * 1024
SPAN = SLOTS * BLK
LOWEST = -1e29
MASKED = -1e30
SCALE = HS ** (-0.5)
VMEM = pl.BlockSpec(memory_space=pltpu.VMEM)
SMEM = pl.BlockSpec(memory_space=pltpu.SMEM)
ANY = pl.BlockSpec(memory_space=pl.ANY)


def kernel_call(body, outs, operands, scalars=0, after=(), scratch=()):
    count = len(operands)

    def run(*refs):
        body(*refs[:count], *refs[count + len(after) :])

    return pl.pallas_call(
        run,
        out_shape=tuple(outs),
        in_specs=[SMEM] * scalars + [VMEM] * (count - scalars) + [ANY] * len(after),
        out_specs=tuple([VMEM] * len(outs)),
        scratch_shapes=list(scratch),
        compiler_params=pltpu.CompilerParams(vmem_limit_bytes=VMEM_LIMIT),
        cost_estimate=pl.CostEstimate(flops=0, bytes_accessed=0, transcendentals=0),
    )(*operands, *after)


def copy_body(value, out):
    out[...] = value[...]


def held(value, *others):
    (copy,) = kernel_call(copy_body, [shape(value.shape, value.dtype)], (value,), after=others)
    return copy


def shape(dims, kind):
    return jax.ShapeDtypeStruct(dims, kind)


def shifted(value, axis, steps):
    count = lax.axis_size(axis)
    return lax.ppermute(
        value, axis, [(s, s + steps) for s in range(max(0, -steps), min(count, count - steps))]
    )


def rolled_pairs(count, far, flip):
    half = count // 2
    return [(((a + far) % half) * 2 + (b ^ flip), a * 2 + b) for a in range(half) for b in range(2)]


def nt(left, right):
    return lax.dot_general(left, right, (((1,), (1,)), ((), ())), preferred_element_type=jnp.float32)


def tn(left, right):
    return lax.dot_general(left, right, (((0,), (0,)), ((), ())), preferred_element_type=jnp.float32)


def nn(left, right):
    return jnp.dot(left, right, preferred_element_type=jnp.float32)


def rules_body(pairs, counts, rules):
    base = lax.axis_index("tm") * QBD
    numbers = lax.broadcasted_iota(jnp.int32, (RULES, BLK), 0)
    values = jnp.zeros((RULES, BLK), jnp.float32)
    for query in range(QBD):
        for back in range(WB):
            hit = jnp.int32(0)
            for row in range(MAXP):
                same = (pairs[row, 0] == base + query) & (pairs[row, 1] == base + query - back)
                hit = hit + jnp.where(same & (row < counts[0]), 1, 0)
            value = jnp.where(hit > 0, 0.0, MASKED).astype(jnp.float32)
            values = jnp.where(numbers == query * WB + back, value, values)
    rules[...] = values


def fill_bias(sets, bias):
    rows = lax.broadcasted_iota(jnp.int32, (BLK, BLK), 0)
    columns = lax.broadcasted_iota(jnp.int32, (BLK, BLK), 1)
    for key in range(QBD):
        for slot in range(SLOTS):
            place = (pl.ds(key * BLK, BLK), pl.ds(slot * BLK, BLK))
            back = slot - key
            if not 0 <= back < WB:
                bias[place] = jnp.full((BLK, BLK), MASKED, jnp.float32)
                continue
            line = (slot % QBD) * WB + back
            block = jnp.broadcast_to(sets[slot // QBD][line : line + 1, :], (BLK, BLK))
            if slot == key:
                block = jnp.where(rows <= columns, block, MASKED)
            bias[place] = block


def head_of(ref, place):
    return ref[:, place * HS : (place + 1) * HS]


def rows_of(own, halo, head, place):
    even, odd, swap, relay, far, flag = halo
    first = head_of(even, place) + head_of(odd, place)
    second = head_of(swap, place) * flag + head_of(relay, place)
    return jnp.concatenate([head_of(own, head), first, second, head_of(far, place)], axis=0)


def halo_of(refs):
    flag = jnp.where(lax.axis_index("tm") % 2 == 0, 1.0, 0.0).astype(jnp.bfloat16)
    return (*refs, flag)


def stats_body(rules, rules1, rules2, q, k, v, g, even, odd, swap, relay, far, own, bias):
    halo = halo_of((even, odd, swap, relay, far))
    fill_bias((rules, rules1, rules2), bias)
    for h in range(H):
        scores = nt(head_of(k, h), rows_of(q, halo, h, h)) * SCALE + bias[...]
        products = nt(head_of(v, h), rows_of(g, halo, h, H + h))
        largest = jnp.maximum(jnp.max(scores, axis=0, keepdims=True), LOWEST)
        weights = jnp.exp(scores - largest)
        own[h : h + 1, :] = largest
        own[H + h : H + h + 1, :] = jnp.sum(weights, axis=0, keepdims=True)
        own[2 * H + h : 2 * H + h + 1, :] = jnp.sum(weights * products, axis=0, keepdims=True)


def spread_body(own, pair, up, down):
    up[:, :BLK] = own[:, 4 * BLK :]
    up[:, BLK:] = pair[:, 2 * BLK :]
    down[:, :BLK] = own[:, :BLK]
    down[:, BLK:] = pair[:, : 3 * BLK]


def merge_stats(own, pair, up, down):
    is_even = lax.axis_index("tm") % 2 == 0

    def terms(ref, first, last):
        part = ref[:, first * BLK : last * BLK]
        large, mass, dot = (part[i * H : (i + 1) * H] for i in range(3))
        return jnp.where(mass > 0, large, LOWEST), mass, dot

    def either(first, second):
        return tuple(jnp.where(is_even, a, b) for a, b in zip(first, second))

    nothing = (
        jnp.full((H, BLK), LOWEST, jnp.float32),
        jnp.zeros((H, BLK), jnp.float32),
        jnp.zeros((H, BLK), jnp.float32),
    )

    def side(*parts):
        return tuple(jnp.concatenate(piece, axis=1) for piece in zip(*parts))

    def cut(part, first, last):
        return tuple(piece[:, first * BLK : last * BLK] for piece in part)

    before = either(terms(up, 1, 4), terms(pair, 2, 5))
    behind = either(terms(pair, 0, 3), terms(down, 1, 4))
    sets = (
        terms(own, 0, SLOTS),
        side(before, cut(behind, 1, 3)),
        side(terms(up, 0, 1), nothing, cut(behind, 0, 1), nothing, terms(down, 0, 1)),
    )
    largest = jnp.maximum(jnp.maximum(sets[0][0], sets[1][0]), sets[2][0])
    mass = jnp.zeros((H, SPAN), jnp.float32)
    dot = jnp.zeros((H, SPAN), jnp.float32)
    for large, part_mass, part_dot in sets:
        factor = jnp.exp(large - largest)
        mass = mass + factor * part_mass
        dot = dot + factor * part_dot
    inverse = jnp.where(mass > 0, 1.0 / jnp.where(mass > 0, mass, 1.0), 0.0)
    return largest, inverse, dot * inverse


def values_body(
    rules, rules1, rules2, q, k, g, even, odd, swap, relay, far, own, pair, up, down, low, total, bias
):
    halo = halo_of((even, odd, swap, relay, far))
    fill_bias((rules, rules1, rules2), bias)
    for index, value in enumerate(merge_stats(own, pair, up, down)):
        total[index * H : (index + 1) * H] = value
    for h in range(H):
        scores = nt(head_of(k, h), rows_of(q, halo, h, h)) * SCALE + bias[...]
        probs = jnp.exp(scores - total[h : h + 1, :]) * total[H + h : H + h + 1, :]
        value_grads = nn(probs.astype(jnp.bfloat16), rows_of(g, halo, h, H + h))
        low[:, h * HS : (h + 1) * HS] = value_grads.astype(jnp.bfloat16)


def keys_body(rules, rules1, rules2, q, k, v, g, even, odd, swap, relay, far, total, low, dq0, dq1, dq2, bias):
    halo = halo_of((even, odd, swap, relay, far))
    fill_bias((rules, rules1, rules2), bias)
    for h in range(H):
        query = rows_of(q, halo, h, h)
        key = head_of(k, h)
        scores = nt(key, query) * SCALE + bias[...]
        products = nt(head_of(v, h), rows_of(g, halo, h, H + h))
        probs = jnp.exp(scores - total[h : h + 1, :]) * total[H + h : H + h + 1, :]
        grad_scores = (probs * (products - total[2 * H + h : 2 * H + h + 1, :])).astype(jnp.bfloat16)
        columns = slice(h * HS, (h + 1) * HS)
        low[:, columns] = (nn(grad_scores, query) * SCALE).astype(jnp.bfloat16)
        grad_query = tn(grad_scores, key) * SCALE
        dq0[:, columns] = grad_query[: 2 * BLK]
        dq1[:, columns] = grad_query[2 * BLK : 4 * BLK].astype(jnp.bfloat16)
        dq2[:, columns] = grad_query[4 * BLK :].astype(jnp.bfloat16)


def cut_body(width, parts, targets, x, *outs):
    for index in range(parts):
        first = pl.multiple_of(targets[index] * width, width)
        outs[index][...] = x[:, pl.ds(first, width)].T


def weight_body(half, parts, y_ref, *refs):
    turned, lows, (send, keep) = refs[:parts], refs[parts : 2 * parts], refs[2 * parts :]
    mine = y_ref[0]
    for out, side in ((send, 1 - mine), (keep, mine)):
        for z in range(0, half, 2):
            places = [pl.ds(pl.multiple_of((2 * place + side) * HS, HS), HS) for place in (z, z + 1)]
            total = None
            for left, low in zip(turned, lows):
                term = nn(left[...], jnp.concatenate([low[:, place] for place in places], axis=1))
                total = term if total is None else total + term
            out[:, z * HS : (z + 2) * HS] = total.astype(out.dtype)


def plain_weight_body(parts, *refs):
    turned, lows, out = refs[:parts], refs[parts : 2 * parts], refs[-1]
    for first in range(0, HD, 2 * HS):
        total = None
        for left, low in zip(turned, lows):
            term = nn(left[...], low[:, first : first + 2 * HS])
            total = term if total is None else total + term
        out[:, first : first + 2 * HS] = total


def rows_body(parts, *refs):
    key_lows, value_lows = refs[:parts], refs[parts : 2 * parts]
    key_weight, value_weight = refs[2 * parts : 2 * parts + 2]
    for key_low, value_low, out in zip(key_lows, value_lows, refs[-parts:]):
        out[...] = (nt(key_low[...], key_weight[...]) + nt(value_low[...], value_weight[...])).astype(out.dtype)


def chunks_body(count, place_ref, keep, heard, *outs):
    for index in range(count):
        columns = pl.ds(pl.multiple_of(place_ref[index] * HS, HS), HS)
        value = keep[:, columns] + heard[:, columns].astype(jnp.float32)
        outs[index][...] = value.astype(outs[index].dtype)


def shards(
    inputs, query_rows, saved_key_rows, value_rows, grad_out, key_weight, value_weight, block_pairs, pair_counts
):
    tokens = query_rows.shape[1]
    n_tm, n_fsdp = lax.axis_size("tm"), lax.axis_size("fsdp")
    shard, owner = lax.axis_index("tm"), lax.axis_index("fsdp")
    d_model = inputs.shape[2]
    rows = d_model // n_fsdp
    half = n_tm // 2
    q, k, v, g = query_rows[0], saved_key_rows[0], value_rows[0], grad_out[0]
    bf16, f32 = jnp.bfloat16, jnp.float32

    first = jnp.concatenate([q[:BLK], g[:BLK]], axis=1)
    latter = jnp.concatenate([q[BLK:], g[BLK:]], axis=1)
    far = shifted(first, "tm", -2)
    swap = lax.ppermute(latter, "tm", rolled_pairs(n_tm, 0, 1))
    even = lax.ppermute(first, "tm", [(2 * z + 1, 2 * z) for z in range(half)])
    (rules,) = kernel_call(rules_body, [shape((RULES, BLK), f32)], (block_pairs[0], pair_counts), scalars=2)
    rules = (rules, shifted(rules, "tm", -1), shifted(rules, "tm", -2))

    relative = [(away, flip) for away in range(n_fsdp // 2) for flip in range(2)]
    parts = len(relative)
    others = [((owner // 2 - away) % (n_fsdp // 2)) * 2 + (owner % 2 ^ flip) for away, flip in relative]
    turned = kernel_call(
        functools.partial(cut_body, rows, parts),
        [shape((rows, tokens), bf16)] * parts,
        (jnp.stack(others), inputs[0]),
        scalars=1,
    )
    turned = [
        lax.ppermute(piece, "fsdp", rolled_pairs(n_fsdp, *place)) if any(place) else piece
        for place, piece in zip(relative, turned)
    ]
    far = held(far, *turned, *rules)
    odd = lax.ppermute(far, "tm", [(2 * z, 2 * z + 1) for z in range(half)])
    relay = lax.ppermute(swap, "tm", [(2 * z + 3, 2 * z + 1) for z in range(half - 1)])

    halo = (even, odd, swap, relay, far)
    bias = pltpu.VMEM((tokens, SPAN), f32)
    (own,) = kernel_call(
        stats_body,
        [shape((3 * H, SPAN), f32)],
        (*rules, q, k, v, g, *halo),
        scratch=[bias],
    )
    pair = lax.ppermute(own, "tm", rolled_pairs(n_tm, 0, 1))
    up, down = kernel_call(spread_body, [shape((3 * H, 4 * BLK), f32)] * 2, (own, pair))
    up, down = shifted(up, "tm", 2), shifted(down, "tm", -2)
    value_low, total = kernel_call(
        values_body,
        [shape((tokens, HD), bf16), shape((3 * H, SPAN), f32)],
        (*rules, q, k, g, *halo, own, pair, up, down),
        scratch=[bias],
    )

    def exchanged(array):
        return lax.ppermute(array, "fsdp", rolled_pairs(n_fsdp, 0, 1))

    def fetched(array):
        return [lax.ppermute(array, "fsdp", rolled_pairs(n_fsdp, away, 0)) for away in range(1, n_fsdp // 2)]

    value_lows = [value_low, exchanged(value_low)]
    value_far = fetched(value_low)
    key_low, dq0, dq1, dq2 = kernel_call(
        keys_body,
        [shape((tokens, HD), kind) for kind in (bf16, f32, bf16)] + [shape((BLK, HD), bf16)],
        (*rules, q, k, v, g, *halo, total),
        scratch=[bias],
    )
    key_lows = [key_low, exchanged(key_low)]
    key_far = fetched(key_low)
    near_terms, far_terms = shifted(dq1, "tm", 1), shifted(dq2, "tm", 2)
    for array in value_far:
        array = held(array, key_low)
        value_lows += [array, exchanged(array)]

    def partial_sums(lows, after=()):
        if HD // n_tm != HS:
            return kernel_call(
                functools.partial(plain_weight_body, parts),
                [shape((rows, HD), f32)],
                (*turned, *lows),
                after=after,
            )
        return kernel_call(
            functools.partial(weight_body, half, parts),
            [shape((rows, HD // 2), bf16), shape((rows, HD // 2), f32)],
            (jnp.reshape(shard % 2, (1,)), *turned, *lows),
            scalars=1,
            after=after,
        )

    def summed(partial):
        if HD // n_tm != HS:
            return lax.psum_scatter(partial[0], "tm", scatter_dimension=1, tiled=True)
        heard = lax.ppermute(partial[0], "tm", rolled_pairs(n_tm, 0, 1))
        places = jnp.stack([(shard // 2 - away) % half for away in range(half)])
        parcels = kernel_call(
            functools.partial(chunks_body, half),
            [shape((rows, HS), f32 if away == 0 else bf16) for away in range(half)],
            (places, partial[1], heard),
            scalars=1,
        )
        result = parcels[0]
        for away in range(1, half):
            result = result + lax.ppermute(parcels[away], "tm", rolled_pairs(n_tm, away, 0)).astype(f32)
        return result

    value_partial = partial_sums(value_lows)
    for array in key_far:
        array = held(array, value_partial[0], near_terms, far_terms)
        key_lows += [array, exchanged(array)]
    key_partial = partial_sums(key_lows)
    value_total, key_total = summed(value_partial), summed(key_partial)
    pieces = kernel_call(
        functools.partial(rows_body, parts),
        [shape((tokens, rows), bf16)] * parts,
        (*key_lows, *value_lows, key_weight, value_weight),
        after=(key_partial[0],),
    )

    result = jnp.zeros((tokens, d_model), bf16)
    for place, source, piece in zip(relative, others, pieces):
        if any(place):
            routes = [(receiver, sender) for sender, receiver in rolled_pairs(n_fsdp, *place)]
            piece = lax.ppermute(piece, "fsdp", routes)
        result = lax.dynamic_update_slice_in_dim(result, piece, source * rows, 1)

    grad_query = dq0 + near_terms.astype(f32)
    grad_query = jnp.concatenate([grad_query[:BLK] + far_terms.astype(f32), grad_query[BLK:]], axis=0).astype(bf16)
    return (grad_query[None], result[None], key_total, value_total)


def solution(mesh):
    return jax.shard_map(
        shards,
        mesh=mesh,
        in_specs=(
            P("fsdp", "tm", None),
            P("fsdp", "tm", None),
            P("fsdp", "tm", None),
            P("fsdp", "tm", None),
            P("fsdp", "tm", None),
            P("fsdp", None),
            P("fsdp", None),
            P("tm", None, None),
            P("tm"),
        ),
        out_specs=(P("fsdp", "tm", None), P("fsdp", "tm", None), P("fsdp", "tm"), P("fsdp", "tm")),
        check_vma=False,
    )
```

```python
import functools

import jax
import jax.numpy as jnp
from jax import lax
from jax.experimental import pallas as pl
from jax.experimental.pallas import tpu as pltpu
from jax.sharding import PartitionSpec as P

H = 8
HS = 128
BLK = 128
HD = 1024
QBD = 2
REACH = 2
MAXP = 8
WB = 4
SLOTS = QBD + WB - 1
UNUSED = 100
CHUNK_FLOPS = 20_000_000_000
VMEM_LIMIT = 16 * 1024 * 1024
SPAN = SLOTS * BLK
LOWEST = -1e29
MASKED = -1e30
SCALE = HS ** (-0.5)
SETS = ((0, 3, 4, 7), (2, 1, 6, 5))
VMEM = pl.BlockSpec(memory_space=pltpu.VMEM)
ANY = pl.BlockSpec(memory_space=pl.ANY)


def kernel_call(body, outs, operands, after=(), scratch=(), flops=1):
    count = len(operands)

    def run(*refs):
        body(*refs[:count], *refs[count + len(after) :])

    return pl.pallas_call(
        run,
        out_shape=tuple(outs),
        in_specs=[VMEM] * count + [ANY] * len(after),
        out_specs=tuple([VMEM] * len(outs)),
        scratch_shapes=list(scratch),
        compiler_params=pltpu.CompilerParams(vmem_limit_bytes=VMEM_LIMIT),
        cost_estimate=pl.CostEstimate(flops=flops, bytes_accessed=1, transcendentals=0),
    )(*operands, *after)


def copy_body(value, out):
    out[...] = value[...]


def held(value, *others):
    (copy,) = kernel_call(copy_body, [shape(value.shape, value.dtype)], (value,), after=others)
    return copy


def shape(dims, kind):
    return jax.ShapeDtypeStruct(dims, kind)


def shifted(value, axis, steps):
    count = lax.axis_size(axis)
    return lax.ppermute(
        value, axis, [(s, s + steps) for s in range(max(0, -steps), min(count, count - steps))]
    )


def rolled_pairs(count, far, flip):
    half = count // 2
    return [(((a + far) % half) * 2 + (b ^ flip), a * 2 + b) for a in range(half) for b in range(2)]


def nt(left, right):
    return lax.dot_general(left, right, (((1,), (1,)), ((), ())), preferred_element_type=jnp.float32)


def tn(left, right):
    return lax.dot_general(left, right, (((0,), (0,)), ((), ())), preferred_element_type=jnp.float32)


def nn(left, right):
    return jnp.dot(left, right, preferred_element_type=jnp.float32)


def rules_of(lines):
    lines = lines.astype(jnp.float32)
    queries, keys = lines[:MAXP], lines[MAXP:]
    found = {}
    for query in range(QBD):
        for back in range(WB):
            hit = jnp.where((queries == query) & (keys == query - back), 0.0, MASKED)
            found[query, back] = jnp.max(hit, axis=0, keepdims=True)
    return found


def fill_bias(own, even, odd, far, bias):
    sets = [rules_of(part) for part in (own[BLK:, :BLK], even[BLK:, :BLK] + odd[BLK:, :BLK], far[BLK:, :BLK])]
    rows = lax.broadcasted_iota(jnp.int32, (BLK, BLK), 0)
    columns = lax.broadcasted_iota(jnp.int32, (BLK, BLK), 1)
    for key in range(QBD):
        for slot in range(SLOTS):
            place = (pl.ds(key * BLK, BLK), pl.ds(slot * BLK, BLK))
            back = slot - key
            if not 0 <= back < WB:
                bias[place] = jnp.full((BLK, BLK), MASKED, jnp.float32)
                continue
            block = jnp.broadcast_to(sets[slot // QBD][slot % QBD, back], (BLK, BLK))
            if slot == key:
                block = jnp.where(rows <= columns, block, MASKED)
            bias[place] = block


def head_of(ref, place):
    return ref[:, place * HS : (place + 1) * HS]


def rows_of(own, halo, head, place):
    even, odd, swap, relay, far, flag = halo
    columns = slice(place * HS, (place + 1) * HS)
    first = even[:BLK, columns] + odd[:BLK, columns]
    second = head_of(swap, place) * flag + head_of(relay, place)
    return jnp.concatenate([head_of(own, head), first, second, far[:BLK, columns]], axis=0)


def halo_of(refs):
    flag = jnp.where(lax.axis_index("tm") % 2 == 0, 1.0, 0.0).astype(jnp.bfloat16)
    return (*refs, flag)


def stats_body(mine, q, k, v, g, even, odd, swap, relay, far, own, bias):
    halo = halo_of((even, odd, swap, relay, far))
    fill_bias(mine, even, odd, far, bias)
    for h in range(H):
        scores = nt(head_of(k, h), rows_of(q, halo, h, h)) * SCALE + bias[...]
        products = nt(head_of(v, h), rows_of(g, halo, h, H + h))
        largest = jnp.maximum(jnp.max(scores, axis=0, keepdims=True), LOWEST)
        weights = jnp.exp(scores - largest)
        own[h : h + 1, :] = largest
        own[H + h : H + h + 1, :] = jnp.sum(weights, axis=0, keepdims=True)
        own[2 * H + h : 2 * H + h + 1, :] = jnp.sum(weights * products, axis=0, keepdims=True)


def spread_body(own, pair, up, down):
    up[:, :BLK] = own[:, 4 * BLK :]
    up[:, BLK:] = pair[:, 2 * BLK :]
    down[:, :BLK] = own[:, :BLK]
    down[:, BLK:] = pair[:, : 3 * BLK]


def merge_stats(own, pair, up, down):
    is_even = lax.axis_index("tm") % 2 == 0

    def terms(ref, first, last):
        part = ref[:, first * BLK : last * BLK]
        large, mass, dot = (part[i * H : (i + 1) * H] for i in range(3))
        return jnp.where(mass > 0, large, LOWEST), mass, dot

    def either(first, second):
        return tuple(jnp.where(is_even, a, b) for a, b in zip(first, second))

    nothing = (
        jnp.full((H, BLK), LOWEST, jnp.float32),
        jnp.zeros((H, BLK), jnp.float32),
        jnp.zeros((H, BLK), jnp.float32),
    )

    def side(*parts):
        return tuple(jnp.concatenate(piece, axis=1) for piece in zip(*parts))

    def cut(part, first, last):
        return tuple(piece[:, first * BLK : last * BLK] for piece in part)

    before = either(terms(up, 1, 4), terms(pair, 2, 5))
    behind = either(terms(pair, 0, 3), terms(down, 1, 4))
    sets = (
        terms(own, 0, SLOTS),
        side(before, cut(behind, 1, 3)),
        side(terms(up, 0, 1), nothing, cut(behind, 0, 1), nothing, terms(down, 0, 1)),
    )
    largest = jnp.maximum(jnp.maximum(sets[0][0], sets[1][0]), sets[2][0])
    mass = jnp.zeros((H, SPAN), jnp.float32)
    dot = jnp.zeros((H, SPAN), jnp.float32)
    for large, part_mass, part_dot in sets:
        factor = jnp.exp(large - largest)
        mass = mass + factor * part_mass
        dot = dot + factor * part_dot
    inverse = jnp.where(mass > 0, 1.0 / jnp.where(mass > 0, mass, 1.0), 0.0)
    return largest, inverse, dot * inverse


def probs_of(h, bias, q, k, halo, total):
    query = rows_of(q, halo, h, h)
    scores = nt(head_of(k, h), query) * SCALE + bias[...]
    return query, jnp.exp(scores - total[h : h + 1, :]) * total[H + h : H + h + 1, :]


def grad_scores_of(h, probs, v, cotangent, total):
    products = nt(head_of(v, h), cotangent)
    return (probs * (products - total[2 * H + h : 2 * H + h + 1, :])).astype(jnp.bfloat16)


def lows_body(bias, q, k, v, g, even, odd, swap, relay, far, own, pair, up, down, mine, other, total):
    halo = halo_of((even, odd, swap, relay, far))
    for index, value in enumerate(merge_stats(own, pair, up, down)):
        total[index * H : (index + 1) * H] = value
    keeps_key = lax.axis_index("fsdp") % 2 == 0
    for place, h in enumerate([h for heads in SETS for h in heads]):
        query, probs = probs_of(h, bias, q, k, halo, total)
        cotangent = rows_of(g, halo, h, H + h)
        value_grads = nn(probs.astype(jnp.bfloat16), cotangent)
        key_grads = nn(grad_scores_of(h, probs, v, cotangent, total), query) * SCALE
        columns = slice(place * HS, (place + 1) * HS)
        mine[:, columns] = jnp.where(keeps_key, key_grads, value_grads).astype(jnp.bfloat16)
        other[:, columns] = jnp.where(keeps_key, value_grads, key_grads).astype(jnp.bfloat16)


def queries_body(bias, q, k, v, g, even, odd, swap, relay, far, total, dq0, dq1, dq2):
    halo = halo_of((even, odd, swap, relay, far))
    for h in range(H):
        _, probs = probs_of(h, bias, q, k, halo, total)
        grad_scores = grad_scores_of(h, probs, v, rows_of(g, halo, h, H + h), total)
        columns = slice(h * HS, (h + 1) * HS)
        grad_query = tn(grad_scores, head_of(k, h)) * SCALE
        dq0[:, columns] = grad_query[: 2 * BLK]
        dq1[:, columns] = grad_query[2 * BLK : 4 * BLK].astype(jnp.bfloat16)
        dq2[:, columns] = grad_query[4 * BLK :].astype(jnp.bfloat16)


def query_body(own, near, far, out):
    total = own[...] + near[...].astype(jnp.float32)
    out[:BLK, :] = (total[:BLK] + far[...].astype(jnp.float32)).astype(jnp.bfloat16)
    out[BLK:, :] = total[BLK:].astype(jnp.bfloat16)


def position(axis):
    index = lax.axis_index(axis)
    return index // 2, index % 2


def turned_back(value, away, count):
    return lax.rem(value + (count - away), count)


def looked_up(table):
    shard = lax.axis_index("tm")
    entry = jnp.int32(table[0])
    for index, value in enumerate(table):
        entry = jnp.where(shard == index, jnp.int32(value), entry)
    return entry


def cut_body(width, x, *outs):
    for away, out in enumerate(outs):
        place = turned_back(position("fsdp")[0], away, len(outs))
        first = pl.multiple_of(place * width, width)
        out[...] = x[:, pl.ds(first, width)].T


def join_body(mine, heard, *outs):
    tokens, width = mine.shape[0], outs[0].shape[1]
    for n, out in enumerate(outs):
        out[:tokens, :] = mine[:, n * width : (n + 1) * width]
        out[tokens:, :] = heard[:, n * width : (n + 1) * width]


def weight_body(pairs, *refs):
    parts = (len(refs) - 2) // 3
    turned, lows, (send, keep) = refs[: 2 * parts], refs[2 * parts : 3 * parts], refs[3 * parts :]
    tokens = turned[0].shape[1]
    mine = position("tm")[1]
    for out, side in ((send, 1 - mine), (keep, mine)):
        for pair in range(0, pairs, 2):
            places = [pl.ds(pl.multiple_of((2 * place + side) * HS, HS), HS) for place in (pair, pair + 1)]
            total = None
            for n, left in enumerate(turned):
                rows = pl.ds(n % 2 * tokens, tokens)
                term = nn(left[...], jnp.concatenate([lows[n // 2][rows, place] for place in places], axis=1))
                total = term if total is None else total + term
            out[:, pair * HS : (pair + 2) * HS] = total.astype(out.dtype)


def plain_weight_body(*refs):
    parts = (len(refs) - 1) // 3
    turned, lows, out = refs[: 2 * parts], refs[2 * parts : 3 * parts], refs[-1]
    tokens = turned[0].shape[1]
    for first in range(0, out.shape[1], 2 * HS):
        total = None
        for n, left in enumerate(turned):
            right = lows[n // 2][n % 2 * tokens : (n % 2 + 1) * tokens, first : first + 2 * HS]
            term = nn(left[...], right)
            total = term if total is None else total + term
        out[:, first : first + 2 * HS] = total


def rows_body(weight, pair_weight, *refs):
    parts = (len(refs) - 2) // len(SETS)
    lows, (keep, send) = refs[:-2], refs[-2:]
    tokens, width = lows[0].shape[0] // 2, weight.shape[0]
    core = position("fsdp")[1]
    order = [h for heads in SETS for h in heads]
    for side, source in ((core, weight), (1 - core, pair_weight)):
        columns = pl.ds(pl.multiple_of(side * width, width), width)
        turned = jnp.concatenate([head_of(source, h) for h in order], axis=1)
        for part in range(parts):
            for flip, out in enumerate((keep, send)):
                rows = pl.ds(flip * tokens, tokens)
                low = jnp.concatenate([lows[n * parts + part][rows, :] for n in range(len(SETS))], axis=1)
                out[part * tokens : (part + 1) * tokens, columns] = nt(low, turned).astype(out.dtype)


def sums_body(keep, heard, *outs):
    tokens = outs[0].shape[0]
    for n, out in enumerate(outs):
        rows = pl.ds(n * tokens, tokens)
        out[...] = (keep[rows, :] + heard[rows, :].astype(jnp.float32)).astype(out.dtype)


def place_body(*refs):
    out = refs[-1]
    for away, piece in enumerate(refs[:-1]):
        width = piece.shape[1]
        place = turned_back(position("fsdp")[0], away, len(refs) - 1)
        out[:, pl.ds(pl.multiple_of(place * width, width), width)] = piece[...]


def chunks_body(tables, keep, heard, *outs):
    for index, table in enumerate(tables):
        columns = pl.ds(pl.multiple_of(looked_up(table) * HS, HS), HS)
        value = keep[:, columns] + heard[:, columns].astype(jnp.float32)
        outs[index][...] = value.astype(outs[index].dtype)


def choose_body(first, second, kept, sent):
    for core, (a, b) in enumerate(((first, second), (second, first))):

        @pl.when(position("fsdp")[1] == core)
        def _():
            kept[...] = a[...]
            sent[...] = b[...]


def total_body(*refs):
    total = None
    for part in refs[:-1]:
        term = part[...].astype(jnp.float32)
        total = term if total is None else total + term
    refs[-1][...] = total


def grouped(refs, sizes):
    groups, start = [], 0
    for size in sizes:
        groups.append(refs[start : start + size])
        start += size
    return groups


def final_body(belongs, sizes, *refs):
    mine, send = refs[-2:]
    height = mine.shape[0]
    core = position("fsdp")[1]
    for n, parts in enumerate(grouped(refs[:-2], sizes)):

        @pl.when(looked_up(belongs) == n)
        def _():
            for out, side in ((mine, core), (send, 1 - core)):
                rows = pl.ds(pl.multiple_of(side * height, height), height)
                total = None
                for part in parts:
                    term = part[rows, :].astype(jnp.float32)
                    total = term if total is None else total + term
                out[...] = total


def shards(
    inputs, query_rows, saved_key_rows, value_rows, grad_out, key_weight, value_weight, block_pairs, pair_counts
):
    tokens = query_rows.shape[1]
    n_tm, n_fsdp = lax.axis_size("tm"), lax.axis_size("fsdp")
    shard, owner = lax.axis_index("tm"), lax.axis_index("fsdp")
    core = owner % 2
    d_model = inputs.shape[2]
    rows = d_model // n_fsdp
    half, chips = n_tm // 2, n_fsdp // 2
    q, k, v, g = query_rows[0], saved_key_rows[0], value_rows[0], grad_out[0]
    bf16, f32 = jnp.bfloat16, jnp.float32

    def exchanged(array):
        return lax.ppermute(array, "fsdp", rolled_pairs(n_fsdp, 0, 1))

    pairs = jnp.where(jnp.arange(MAXP)[:, None] < pair_counts[0], block_pairs[0] - shard * QBD, UNUSED)
    lines = jnp.broadcast_to(pairs.T.reshape(2 * MAXP, 1), (2 * MAXP, 2 * HD)).astype(bf16)
    first = jnp.concatenate([jnp.concatenate([q[:BLK], g[:BLK]], axis=1), lines], axis=0)
    latter = jnp.concatenate([q[BLK:], g[BLK:]], axis=1)
    far = shifted(first, "tm", -2)
    swap = lax.ppermute(latter, "tm", rolled_pairs(n_tm, 0, 1))
    even = lax.ppermute(first, "tm", [(2 * z + 1, 2 * z) for z in range(half)])
    odd = lax.ppermute(far, "tm", [(2 * z, 2 * z + 1) for z in range(half)])
    relay = lax.ppermute(swap, "tm", [(2 * z + 3, 2 * z + 1) for z in range(half - 1)])

    cuts = kernel_call(
        functools.partial(cut_body, 2 * rows),
        [shape((2 * rows, tokens), bf16)] * chips,
        (inputs[0],),
    )
    turned = []
    for away, piece in enumerate(cuts):
        if away:
            piece = lax.ppermute(piece, "fsdp", rolled_pairs(n_fsdp, away, 0))
        turned += [piece, exchanged(piece)]

    halo = (even, odd, swap, relay, far)
    own, bias = kernel_call(
        stats_body,
        [shape((3 * H, SPAN), f32), shape((tokens, SPAN), f32)],
        (first, q, k, v, g, *halo),
        after=turned,
    )
    pair = lax.ppermute(own, "tm", rolled_pairs(n_tm, 0, 1))
    up, down = kernel_call(spread_body, [shape((3 * H, 4 * BLK), f32)] * 2, (own, pair))
    up, down = shifted(up, "tm", 2), shifted(down, "tm", -2)
    mine, other, total = kernel_call(
        lows_body,
        [shape((tokens, HD), bf16), shape((tokens, HD), bf16), shape((3 * H, SPAN), f32)],
        (bias, q, k, v, g, *halo, own, pair, up, down),
    )
    heard = exchanged(other)
    widths = [len(heads) * HS for heads in SETS]
    lows = kernel_call(join_body, [shape((2 * tokens, width), bf16) for width in widths], (mine, heard))
    far_lows = [
        [lax.ppermute(low, "fsdp", rolled_pairs(n_fsdp, away, 0)) for away in range(1, chips)] for low in lows
    ]
    dq0, dq1, dq2 = kernel_call(
        queries_body,
        [shape((tokens, HD), f32), shape((tokens, HD), bf16), shape((BLK, HD), bf16)],
        (bias, q, k, v, g, *halo, total),
        after=lows,
    )
    near_terms, far_terms = shifted(dq1, "tm", 1), shifted(dq2, "tm", 2)

    aligned = HD // n_tm == HS
    groups, partials = [], []
    for heads, low, arrays, width in zip(SETS, lows, far_lows, widths):
        if partials:
            arrays = [held(array, partials[-1][0], near_terms, far_terms) for array in arrays]
        group = (low, *arrays)
        groups.append(group)
        if aligned:
            partials.append(
                kernel_call(
                    functools.partial(weight_body, len(heads) // 2),
                    [shape((2 * rows, width // 2), bf16), shape((2 * rows, width // 2), f32)],
                    (*turned, *group),
                )
            )
        else:
            partials.append(kernel_call(plain_weight_body, [shape((2 * rows, width), f32)], (*turned, *group)))
    weight, pair_weight = kernel_call(
        choose_body, [shape(key_weight.shape, bf16)] * 2, (key_weight, value_weight)
    )
    pair_weight = exchanged(pair_weight)
    keep, send = kernel_call(
        rows_body,
        [shape((chips * tokens, 2 * rows), kind) for kind in (f32, bf16)],
        (weight, pair_weight, *(array for group in groups for array in group)),
        after=(partials[-1][0],),
    )
    pieces = kernel_call(sums_body, [shape((tokens, 2 * rows), bf16)] * chips, (keep, exchanged(send)))
    arrived = []
    for away, piece in enumerate(pieces):
        if away:
            routes = [(receiver, sender) for sender, receiver in rolled_pairs(n_fsdp, away, 0)]
            piece = lax.ppermute(piece, "fsdp", routes)
        arrived.append(piece)
    (result,) = kernel_call(place_body, [shape((tokens, d_model), bf16)], arrived)
    (grad_query,) = kernel_call(query_body, [shape((tokens, HD), bf16)], (dq0, near_terms, far_terms))

    if aligned:
        sums, earlier = [], ()
        for index, (heads, (send, keep)) in enumerate(zip(SETS, partials)):
            pairs_here = len(heads) // 2
            partner = lax.ppermute(send, "tm", rolled_pairs(n_tm, 0, 1))
            goal = [[heads[2 * n + y] // 2 for n in range(pairs_here)] for y in range(2)]
            tables = []
            for away in range(half):
                tables.append([0] * n_tm)
                for y in range(2):
                    for n, z in enumerate(goal[y]):
                        tables[-1][((z + away) % half) * 2 + y] = n
            chunks = kernel_call(
                functools.partial(chunks_body, tables),
                [shape((2 * rows, HS), f32 if away == 0 else bf16) for away in range(half)],
                (keep, partner),
                after=earlier,
                flops=CHUNK_FLOPS if index == 0 else 1,
            )
            parcels = [chunks[0]]
            for away in range(1, half):
                routes = [(((z + away) % half) * 2 + y, z * 2 + y) for y in range(2) for z in goal[y]]
                parcels.append(lax.ppermute(chunks[away], "tm", routes))
            if index < len(SETS) - 1:
                parcels = kernel_call(total_body, [shape((2 * rows, HS), f32)], parcels)
            earlier = (*parcels, *pieces)
            sums.append(parcels)
    if aligned:
        belongs = [[j in heads for heads in SETS].index(True) for j in range(n_tm)]
        ours, theirs = kernel_call(
            functools.partial(final_body, belongs, [len(parcels) for parcels in sums]),
            [shape((rows, HS), f32)] * 2,
            [parcel for parcels in sums for parcel in parcels],
            after=(result, grad_query),
        )
    else:
        order = [h for heads in SETS for h in heads]
        partial = jnp.concatenate([part[0] for part in partials], axis=1)
        partial = jnp.concatenate([partial[:, order.index(h) * HS : (order.index(h) + 1) * HS] for h in range(H)], axis=1)
        whole = lax.psum_scatter(partial, "tm", scatter_dimension=1, tiled=True)
        ours, theirs = (lax.dynamic_slice_in_dim(whole, side * rows, rows, 0) for side in (core, 1 - core))
    key_total, value_total = kernel_call(
        choose_body, [shape(ours.shape, f32)] * 2, (ours, exchanged(theirs))
    )

    return (grad_query[None], result[None], key_total, value_total)


def solution(mesh):
    return jax.shard_map(
        shards,
        mesh=mesh,
        in_specs=(
            P("fsdp", "tm", None),
            P("fsdp", "tm", None),
            P("fsdp", "tm", None),
            P("fsdp", "tm", None),
            P("fsdp", "tm", None),
            P("fsdp", None),
            P("fsdp", None),
            P("tm", None, None),
            P("tm"),
        ),
        out_specs=(P("fsdp", "tm", None), P("fsdp", "tm", None), P("fsdp", "tm"), P("fsdp", "tm")),
        check_vma=False,
    )
```

```python
import functools

import jax
import jax.numpy as jnp
from jax import lax
from jax.experimental import pallas as pl
from jax.experimental.pallas import tpu as pltpu
from jax.sharding import PartitionSpec as P

H = 8
HS = 128
BLK = 128
HD = 1024
QBD = 2
REACH = 2
MAXP = 8
WB = 4
SLOTS = QBD + WB - 1
UNUSED = 100
CHUNK_FLOPS = 20_000_000_000
VMEM_LIMIT = 16 * 1024 * 1024
SPAN = SLOTS * BLK
LOWEST = -1e29
MASKED = -1e30
SCALE = HS ** (-0.5)
SETS = ((0, 3, 4, 7), (2, 1, 6, 5))
VMEM = pl.BlockSpec(memory_space=pltpu.VMEM)
ANY = pl.BlockSpec(memory_space=pl.ANY)


def kernel_call(body, outs, operands, after=(), scratch=(), flops=1):
    count = len(operands)

    def run(*refs):
        body(*refs[:count], *refs[count + len(after) :])

    return pl.pallas_call(
        run,
        out_shape=tuple(outs),
        in_specs=[VMEM] * count + [ANY] * len(after),
        out_specs=tuple([VMEM] * len(outs)),
        scratch_shapes=list(scratch),
        compiler_params=pltpu.CompilerParams(vmem_limit_bytes=VMEM_LIMIT),
        cost_estimate=pl.CostEstimate(flops=flops, bytes_accessed=1, transcendentals=0),
    )(*operands, *after)


def copy_body(value, out):
    out[...] = value[...]


def held(value, *others):
    (copy,) = kernel_call(copy_body, [shape(value.shape, value.dtype)], (value,), after=others)
    return copy


def shape(dims, kind):
    return jax.ShapeDtypeStruct(dims, kind)


def shifted(value, axis, steps):
    count = lax.axis_size(axis)
    return lax.ppermute(
        value, axis, [(s, s + steps) for s in range(max(0, -steps), min(count, count - steps))]
    )


def rolled_pairs(count, far, flip):
    half = count // 2
    return [(((a + far) % half) * 2 + (b ^ flip), a * 2 + b) for a in range(half) for b in range(2)]


def nt(left, right):
    return lax.dot_general(left, right, (((1,), (1,)), ((), ())), preferred_element_type=jnp.float32)


def tn(left, right):
    return lax.dot_general(left, right, (((0,), (0,)), ((), ())), preferred_element_type=jnp.float32)


def nn(left, right):
    return jnp.dot(left, right, preferred_element_type=jnp.float32)


def rules_of(lines):
    lines = lines.astype(jnp.float32)
    queries, keys = lines[:MAXP], lines[MAXP:]
    found = {}
    for query in range(QBD):
        for back in range(WB):
            hit = jnp.where((queries == query) & (keys == query - back), 0.0, MASKED)
            found[query, back] = jnp.max(hit, axis=0, keepdims=True)
    return found


def fill_bias(own, even, odd, far, bias):
    sets = [rules_of(part) for part in (own[BLK:, :BLK], even[BLK:, :BLK] + odd[BLK:, :BLK], far[BLK:, :BLK])]
    rows = lax.broadcasted_iota(jnp.int32, (BLK, BLK), 0)
    columns = lax.broadcasted_iota(jnp.int32, (BLK, BLK), 1)
    for key in range(QBD):
        for slot in range(SLOTS):
            place = (pl.ds(key * BLK, BLK), pl.ds(slot * BLK, BLK))
            back = slot - key
            if not 0 <= back < WB:
                bias[place] = jnp.full((BLK, BLK), MASKED, jnp.float32)
                continue
            block = jnp.broadcast_to(sets[slot // QBD][slot % QBD, back], (BLK, BLK))
            if slot == key:
                block = jnp.where(rows <= columns, block, MASKED)
            bias[place] = block


def head_of(ref, place):
    return ref[:, place * HS : (place + 1) * HS]


def rows_of(own, halo, head, place):
    even, odd, swap, relay, far, flag = halo
    columns = slice(place * HS, (place + 1) * HS)
    first = even[:BLK, columns] + odd[:BLK, columns]
    second = head_of(swap, place) * flag + head_of(relay, place)
    return jnp.concatenate([head_of(own, head), first, second, far[:BLK, columns]], axis=0)


def halo_of(refs):
    flag = jnp.where(lax.axis_index("tm") % 2 == 0, 1.0, 0.0).astype(jnp.bfloat16)
    return (*refs, flag)


def stats_body(mine, q, k, v, g, even, odd, swap, relay, far, own, bias):
    halo = halo_of((even, odd, swap, relay, far))
    fill_bias(mine, even, odd, far, bias)
    for h in range(H):
        scores = nt(head_of(k, h), rows_of(q, halo, h, h)) * SCALE + bias[...]
        products = nt(head_of(v, h), rows_of(g, halo, h, H + h))
        largest = jnp.maximum(jnp.max(scores, axis=0, keepdims=True), LOWEST)
        weights = jnp.exp(scores - largest)
        own[h : h + 1, :] = largest
        own[H + h : H + h + 1, :] = jnp.sum(weights, axis=0, keepdims=True)
        own[2 * H + h : 2 * H + h + 1, :] = jnp.sum(weights * products, axis=0, keepdims=True)


def spread_body(own, pair, up, down):
    up[:, :BLK] = own[:, 4 * BLK :]
    up[:, BLK:] = pair[:, 2 * BLK :]
    down[:, :BLK] = own[:, :BLK]
    down[:, BLK:] = pair[:, : 3 * BLK]


def merge_stats(own, pair, up, down):
    is_even = lax.axis_index("tm") % 2 == 0

    def terms(ref, first, last):
        part = ref[:, first * BLK : last * BLK]
        large, mass, dot = (part[i * H : (i + 1) * H] for i in range(3))
        return jnp.where(mass > 0, large, LOWEST), mass, dot

    def either(first, second):
        return tuple(jnp.where(is_even, a, b) for a, b in zip(first, second))

    nothing = (
        jnp.full((H, BLK), LOWEST, jnp.float32),
        jnp.zeros((H, BLK), jnp.float32),
        jnp.zeros((H, BLK), jnp.float32),
    )

    def side(*parts):
        return tuple(jnp.concatenate(piece, axis=1) for piece in zip(*parts))

    def cut(part, first, last):
        return tuple(piece[:, first * BLK : last * BLK] for piece in part)

    before = either(terms(up, 1, 4), terms(pair, 2, 5))
    behind = either(terms(pair, 0, 3), terms(down, 1, 4))
    sets = (
        terms(own, 0, SLOTS),
        side(before, cut(behind, 1, 3)),
        side(terms(up, 0, 1), nothing, cut(behind, 0, 1), nothing, terms(down, 0, 1)),
    )
    largest = jnp.maximum(jnp.maximum(sets[0][0], sets[1][0]), sets[2][0])
    mass = jnp.zeros((H, SPAN), jnp.float32)
    dot = jnp.zeros((H, SPAN), jnp.float32)
    for large, part_mass, part_dot in sets:
        factor = jnp.exp(large - largest)
        mass = mass + factor * part_mass
        dot = dot + factor * part_dot
    inverse = jnp.where(mass > 0, 1.0 / jnp.where(mass > 0, mass, 1.0), 0.0)
    return largest, inverse, dot * inverse


def probs_of(h, bias, q, k, halo, total):
    query = rows_of(q, halo, h, h)
    scores = nt(head_of(k, h), query) * SCALE + bias[...]
    return query, jnp.exp(scores - total[h : h + 1, :]) * total[H + h : H + h + 1, :]


def grad_scores_of(h, probs, v, cotangent, total):
    products = nt(head_of(v, h), cotangent)
    return (probs * (products - total[2 * H + h : 2 * H + h + 1, :])).astype(jnp.bfloat16)


def lows_body(bias, q, k, v, g, even, odd, swap, relay, far, own, pair, up, down, mine, other, total):
    halo = halo_of((even, odd, swap, relay, far))
    for index, value in enumerate(merge_stats(own, pair, up, down)):
        total[index * H : (index + 1) * H] = value
    keeps_key = lax.axis_index("fsdp") % 2 == 0
    for place, h in enumerate([h for heads in SETS for h in heads]):
        query, probs = probs_of(h, bias, q, k, halo, total)
        cotangent = rows_of(g, halo, h, H + h)
        value_grads = nn(probs.astype(jnp.bfloat16), cotangent)
        key_grads = nn(grad_scores_of(h, probs, v, cotangent, total), query) * SCALE
        columns = slice(place * HS, (place + 1) * HS)
        mine[:, columns] = jnp.where(keeps_key, key_grads, value_grads).astype(jnp.bfloat16)
        other[:, columns] = jnp.where(keeps_key, value_grads, key_grads).astype(jnp.bfloat16)


def queries_body(bias, q, k, v, g, even, odd, swap, relay, far, total, dq0, dq1, dq2):
    halo = halo_of((even, odd, swap, relay, far))
    for h in range(H):
        _, probs = probs_of(h, bias, q, k, halo, total)
        grad_scores = grad_scores_of(h, probs, v, rows_of(g, halo, h, H + h), total)
        columns = slice(h * HS, (h + 1) * HS)
        grad_query = tn(grad_scores, head_of(k, h)) * SCALE
        dq0[:, columns] = grad_query[: 2 * BLK]
        dq1[:, columns] = grad_query[2 * BLK : 4 * BLK].astype(jnp.bfloat16)
        dq2[:, columns] = grad_query[4 * BLK :].astype(jnp.bfloat16)


def query_body(own, near, far, out):
    total = own[...] + near[...].astype(jnp.float32)
    out[:BLK, :] = (total[:BLK] + far[...].astype(jnp.float32)).astype(jnp.bfloat16)
    out[BLK:, :] = total[BLK:].astype(jnp.bfloat16)


def position(axis):
    index = lax.axis_index(axis)
    return index // 2, index % 2


def turned_back(value, away, count):
    return lax.rem(value + (count - away), count)


def looked_up(table):
    shard = lax.axis_index("tm")
    entry = jnp.int32(table[0])
    for index, value in enumerate(table):
        entry = jnp.where(shard == index, jnp.int32(value), entry)
    return entry


def cut_body(width, x, *outs):
    for away, out in enumerate(outs):
        place = turned_back(position("fsdp")[0], away, len(outs))
        first = pl.multiple_of(place * width, width)
        out[...] = x[:, pl.ds(first, width)].T


def join_body(mine, heard, *outs):
    tokens, width = mine.shape[0], outs[0].shape[1]
    for n, out in enumerate(outs):
        out[:tokens, :] = mine[:, n * width : (n + 1) * width]
        out[tokens:, :] = heard[:, n * width : (n + 1) * width]


def weight_body(pairs, *refs):
    parts = (len(refs) - 2) // 3
    turned, lows, (send, keep) = refs[: 2 * parts], refs[2 * parts : 3 * parts], refs[3 * parts :]
    tokens = turned[0].shape[1]
    mine = position("tm")[1]
    for out, side in ((send, 1 - mine), (keep, mine)):
        for pair in range(0, pairs, 2):
            places = [pl.ds(pl.multiple_of((2 * place + side) * HS, HS), HS) for place in (pair, pair + 1)]
            total = None
            for n, left in enumerate(turned):
                rows = pl.ds(n % 2 * tokens, tokens)
                term = nn(left[...], jnp.concatenate([lows[n // 2][rows, place] for place in places], axis=1))
                total = term if total is None else total + term
            out[:, pair * HS : (pair + 2) * HS] = total.astype(out.dtype)


def plain_weight_body(*refs):
    parts = (len(refs) - 1) // 3
    turned, lows, out = refs[: 2 * parts], refs[2 * parts : 3 * parts], refs[-1]
    tokens = turned[0].shape[1]
    for first in range(0, out.shape[1], 2 * HS):
        total = None
        for n, left in enumerate(turned):
            right = lows[n // 2][n % 2 * tokens : (n % 2 + 1) * tokens, first : first + 2 * HS]
            term = nn(left[...], right)
            total = term if total is None else total + term
        out[:, first : first + 2 * HS] = total


def rows_body(weight, pair_weight, *refs):
    parts = (len(refs) - 2) // len(SETS)
    lows, (keep, send) = refs[:-2], refs[-2:]
    tokens, width = lows[0].shape[0] // 2, weight.shape[0]
    core = position("fsdp")[1]
    order = [h for heads in SETS for h in heads]
    for side, source in ((core, weight), (1 - core, pair_weight)):
        columns = pl.ds(pl.multiple_of(side * width, width), width)
        turned = jnp.concatenate([head_of(source, h) for h in order], axis=1)
        for part in range(parts):
            for flip, out in enumerate((keep, send)):
                rows = pl.ds(flip * tokens, tokens)
                low = jnp.concatenate([lows[n * parts + part][rows, :] for n in range(len(SETS))], axis=1)
                out[part * tokens : (part + 1) * tokens, columns] = nt(low, turned).astype(out.dtype)


def sums_body(keep, heard, *outs):
    tokens = outs[0].shape[0]
    for n, out in enumerate(outs):
        rows = pl.ds(n * tokens, tokens)
        out[...] = (keep[rows, :] + heard[rows, :].astype(jnp.float32)).astype(out.dtype)


def place_body(*refs):
    out = refs[-1]
    for away, piece in enumerate(refs[:-1]):
        width = piece.shape[1]
        place = turned_back(position("fsdp")[0], away, len(refs) - 1)
        out[:, pl.ds(pl.multiple_of(place * width, width), width)] = piece[...]


def chunks_body(tables, keep, heard, *outs):
    for index, table in enumerate(tables):
        columns = pl.ds(pl.multiple_of(looked_up(table) * HS, HS), HS)
        value = keep[:, columns] + heard[:, columns].astype(jnp.float32)
        outs[index][...] = value.astype(outs[index].dtype)


def choose_body(first, second, kept, sent):
    for core, (a, b) in enumerate(((first, second), (second, first))):

        @pl.when(position("fsdp")[1] == core)
        def _():
            kept[...] = a[...]
            sent[...] = b[...]


def grouped(refs, sizes):
    groups, start = [], 0
    for size in sizes:
        groups.append(refs[start : start + size])
        start += size
    return groups


def final_body(belongs, sizes, *refs):
    mine, send = refs[-2:]
    height = mine.shape[0]
    core = position("fsdp")[1]
    for n, parts in enumerate(grouped(refs[:-2], sizes)):

        @pl.when(looked_up(belongs) == n)
        def _():
            for out, side in ((mine, core), (send, 1 - core)):
                rows = pl.ds(pl.multiple_of(side * height, height), height)
                total = None
                for part in parts:
                    term = part[rows, :].astype(jnp.float32)
                    total = term if total is None else total + term
                out[...] = total


def shards(
    inputs, query_rows, saved_key_rows, value_rows, grad_out, key_weight, value_weight, block_pairs, pair_counts
):
    tokens = query_rows.shape[1]
    n_tm, n_fsdp = lax.axis_size("tm"), lax.axis_size("fsdp")
    shard, owner = lax.axis_index("tm"), lax.axis_index("fsdp")
    core = owner % 2
    d_model = inputs.shape[2]
    rows = d_model // n_fsdp
    half, chips = n_tm // 2, n_fsdp // 2
    q, k, v, g = query_rows[0], saved_key_rows[0], value_rows[0], grad_out[0]
    bf16, f32 = jnp.bfloat16, jnp.float32

    def exchanged(array):
        return lax.ppermute(array, "fsdp", rolled_pairs(n_fsdp, 0, 1))

    pairs = jnp.where(jnp.arange(MAXP)[:, None] < pair_counts[0], block_pairs[0] - shard * QBD, UNUSED)
    lines = jnp.broadcast_to(pairs.T.reshape(2 * MAXP, 1), (2 * MAXP, 2 * HD)).astype(bf16)
    first = jnp.concatenate([jnp.concatenate([q[:BLK], g[:BLK]], axis=1), lines], axis=0)
    latter = jnp.concatenate([q[BLK:], g[BLK:]], axis=1)
    far = shifted(first, "tm", -2)
    swap = lax.ppermute(latter, "tm", rolled_pairs(n_tm, 0, 1))
    even = lax.ppermute(first, "tm", [(2 * z + 1, 2 * z) for z in range(half)])
    odd = lax.ppermute(far, "tm", [(2 * z, 2 * z + 1) for z in range(half)])
    relay = lax.ppermute(swap, "tm", [(2 * z + 3, 2 * z + 1) for z in range(half - 1)])

    cuts = kernel_call(
        functools.partial(cut_body, 2 * rows),
        [shape((2 * rows, tokens), bf16)] * chips,
        (inputs[0],),
    )
    turned = []
    for away, piece in enumerate(cuts):
        if away:
            piece = lax.ppermute(piece, "fsdp", rolled_pairs(n_fsdp, away, 0))
        turned += [piece, exchanged(piece)]

    halo = (even, odd, swap, relay, far)
    own, bias = kernel_call(
        stats_body,
        [shape((3 * H, SPAN), f32), shape((tokens, SPAN), f32)],
        (first, q, k, v, g, *halo),
        after=turned,
    )
    pair = lax.ppermute(own, "tm", rolled_pairs(n_tm, 0, 1))
    up, down = kernel_call(spread_body, [shape((3 * H, 4 * BLK), f32)] * 2, (own, pair))
    up, down = shifted(up, "tm", 2), shifted(down, "tm", -2)
    mine, other, total = kernel_call(
        lows_body,
        [shape((tokens, HD), bf16), shape((tokens, HD), bf16), shape((3 * H, SPAN), f32)],
        (bias, q, k, v, g, *halo, own, pair, up, down),
    )
    heard = exchanged(other)
    widths = [len(heads) * HS for heads in SETS]
    lows = kernel_call(join_body, [shape((2 * tokens, width), bf16) for width in widths], (mine, heard))
    far_lows = [
        [lax.ppermute(low, "fsdp", rolled_pairs(n_fsdp, away, 0)) for away in range(1, chips)] for low in lows
    ]
    dq0, dq1, dq2 = kernel_call(
        queries_body,
        [shape((tokens, HD), f32), shape((tokens, HD), bf16), shape((BLK, HD), bf16)],
        (bias, q, k, v, g, *halo, total),
        after=lows,
    )
    near_terms, far_terms = shifted(dq1, "tm", 1), shifted(dq2, "tm", 2)

    aligned = HD // n_tm == HS
    groups, partials = [], []
    for heads, low, arrays, width in zip(SETS, lows, far_lows, widths):
        if partials:
            arrays = [held(array, partials[-1][0], near_terms, far_terms) for array in arrays]
        group = (low, *arrays)
        groups.append(group)
        if aligned:
            partials.append(
                kernel_call(
                    functools.partial(weight_body, len(heads) // 2),
                    [shape((2 * rows, width // 2), bf16), shape((2 * rows, width // 2), f32)],
                    (*turned, *group),
                )
            )
        else:
            partials.append(kernel_call(plain_weight_body, [shape((2 * rows, width), f32)], (*turned, *group)))
    weight, pair_weight = kernel_call(
        choose_body, [shape(key_weight.shape, bf16)] * 2, (key_weight, value_weight)
    )
    pair_weight = exchanged(pair_weight)
    keep, send = kernel_call(
        rows_body,
        [shape((chips * tokens, 2 * rows), kind) for kind in (f32, bf16)],
        (weight, pair_weight, *(array for group in groups for array in group)),
        after=(partials[-1][0],),
    )
    pieces = kernel_call(sums_body, [shape((tokens, 2 * rows), bf16)] * chips, (keep, exchanged(send)))
    arrived = []
    for away, piece in enumerate(pieces):
        if away:
            routes = [(receiver, sender) for sender, receiver in rolled_pairs(n_fsdp, away, 0)]
            piece = lax.ppermute(piece, "fsdp", routes)
        arrived.append(piece)
    (result,) = kernel_call(place_body, [shape((tokens, d_model), bf16)], arrived)
    (grad_query,) = kernel_call(query_body, [shape((tokens, HD), bf16)], (dq0, near_terms, far_terms))

    if aligned:
        sums = []
        for index, (heads, (send, keep)) in enumerate(zip(SETS, partials)):
            pairs_here = len(heads) // 2
            partner = lax.ppermute(send, "tm", rolled_pairs(n_tm, 0, 1))
            goal = [[heads[2 * n + y] // 2 for n in range(pairs_here)] for y in range(2)]
            tables = []
            for away in range(half):
                tables.append([0] * n_tm)
                for y in range(2):
                    for n, z in enumerate(goal[y]):
                        tables[-1][((z + away) % half) * 2 + y] = n
            chunks = kernel_call(
                functools.partial(chunks_body, tables),
                [shape((2 * rows, HS), f32 if away == 0 else bf16) for away in range(half)],
                (keep, partner),
                after=pieces if index else (),
                flops=CHUNK_FLOPS,
            )
            parcels = [chunks[0]]
            for away in range(1, half):
                routes = [(((z + away) % half) * 2 + y, z * 2 + y) for y in range(2) for z in goal[y]]
                parcels.append(lax.ppermute(chunks[away], "tm", routes))
            sums.append(parcels)
    if aligned:
        belongs = [[j in heads for heads in SETS].index(True) for j in range(n_tm)]
        ours, theirs = kernel_call(
            functools.partial(final_body, belongs, [len(parcels) for parcels in sums]),
            [shape((rows, HS), f32)] * 2,
            [parcel for parcels in sums for parcel in parcels],
            after=(result, grad_query),
        )
    else:
        order = [h for heads in SETS for h in heads]
        partial = jnp.concatenate([part[0] for part in partials], axis=1)
        partial = jnp.concatenate([partial[:, order.index(h) * HS : (order.index(h) + 1) * HS] for h in range(H)], axis=1)
        whole = lax.psum_scatter(partial, "tm", scatter_dimension=1, tiled=True)
        ours, theirs = (lax.dynamic_slice_in_dim(whole, side * rows, rows, 0) for side in (core, 1 - core))
    key_total, value_total = kernel_call(
        choose_body, [shape(ours.shape, f32)] * 2, (ours, exchanged(theirs))
    )

    return (grad_query[None], result[None], key_total, value_total)


def solution(mesh):
    return jax.shard_map(
        shards,
        mesh=mesh,
        in_specs=(
            P("fsdp", "tm", None),
            P("fsdp", "tm", None),
            P("fsdp", "tm", None),
            P("fsdp", "tm", None),
            P("fsdp", "tm", None),
            P("fsdp", None),
            P("fsdp", None),
            P("tm", None, None),
            P("tm"),
        ),
        out_specs=(P("fsdp", "tm", None), P("fsdp", "tm", None), P("fsdp", "tm"), P("fsdp", "tm")),
        check_vma=False,
    )
```

```python
import functools

import jax
import jax.numpy as jnp
from jax import lax
from jax.experimental import pallas as pl
from jax.experimental.pallas import tpu as pltpu
from jax.sharding import PartitionSpec as P

H = 8
HS = 128
BLK = 128
HD = 1024
QBD = 2
REACH = 2
MAXP = 8
WB = 4
SLOTS = QBD + WB - 1
UNUSED = 100
STATS_FLOPS = 20_000_000_000
WEIGHT_FLOPS = 1
VMEM_LIMIT = 16 * 1024 * 1024
SPAN = SLOTS * BLK
LOWEST = -1e29
MASKED = -1e30
SCALE = HS ** (-0.5)
SETS = ((0, 3), (1, 2))
ORDER = tuple(n for members in SETS for n in members)
KEPT = len(ORDER)
WIDE = KEPT * HS
HALO = WB - 1
WINDOW = (2 * QBD + HALO) * BLK
LINES = 2 * MAXP
VMEM = pl.BlockSpec(memory_space=pltpu.VMEM)
ANY = pl.BlockSpec(memory_space=pl.ANY)


def kernel_call(body, outs, operands, after=(), scratch=(), flops=1):
    count = len(operands)

    def run(*refs):
        body(*refs[:count], *refs[count + len(after) :])

    return pl.pallas_call(
        run,
        out_shape=tuple(outs),
        in_specs=[VMEM] * count + [ANY] * len(after),
        out_specs=tuple([VMEM] * len(outs)),
        scratch_shapes=list(scratch),
        compiler_params=pltpu.CompilerParams(vmem_limit_bytes=VMEM_LIMIT),
        cost_estimate=pl.CostEstimate(flops=flops, bytes_accessed=1, transcendentals=0),
    )(*operands, *after)


def copy_body(value, out):
    out[...] = value[...]


def held(value, *others):
    (copy,) = kernel_call(copy_body, [shape(value.shape, value.dtype)], (value,), after=others)
    return copy


def shape(dims, kind):
    return jax.ShapeDtypeStruct(dims, kind)


def shifted(value, axis, steps):
    count = lax.axis_size(axis)
    return lax.ppermute(
        value, axis, [(s, s + steps) for s in range(max(0, -steps), min(count, count - steps))]
    )


def rolled_pairs(count, far, flip):
    half = count // 2
    return [(((a + far) % half) * 2 + (b ^ flip), a * 2 + b) for a in range(half) for b in range(2)]


def nt(left, right):
    return lax.dot_general(left, right, (((1,), (1,)), ((), ())), preferred_element_type=jnp.float32)


def tn(left, right):
    return lax.dot_general(left, right, (((0,), (0,)), ((), ())), preferred_element_type=jnp.float32)


def nn(left, right):
    return jnp.dot(left, right, preferred_element_type=jnp.float32)


def rules_of(lines):
    lines = lines.astype(jnp.float32)
    queries, keys = lines[:MAXP], lines[MAXP:]
    found = {}
    for query in range(QBD):
        for back in range(WB):
            hit = jnp.where((queries == query) & (keys == query - back), 0.0, MASKED)
            found[query, back] = jnp.max(hit, axis=0, keepdims=True)
    return found


def fill_bias(sets, bias):
    rows = lax.broadcasted_iota(jnp.int32, (BLK, BLK), 0)
    columns = lax.broadcasted_iota(jnp.int32, (BLK, BLK), 1)
    for key in range(QBD):
        for slot in range(SLOTS):
            place = (pl.ds(key * BLK, BLK), pl.ds(slot * BLK, BLK))
            back = slot - key
            if not 0 <= back < WB:
                bias[place] = jnp.full((BLK, BLK), MASKED, jnp.float32)
                continue
            block = jnp.broadcast_to(sets[slot // QBD][slot % QBD, back], (BLK, BLK))
            if slot == key:
                block = jnp.where(rows <= columns, block, MASKED)
            bias[place] = block


def position(axis):
    index = lax.axis_index(axis)
    return index // 2, index % 2


def lanes(index):
    return pl.ds(pl.multiple_of(index * HS, HS), HS)


def split_body(*refs):
    first, second = refs[-4:-2]
    kept, sent = refs[-2:]
    parity = position("tm")[1]
    for side, array in enumerate((first, second)):
        for place, n in enumerate(ORDER):
            columns = slice((side * KEPT + place) * HS, (side * KEPT + place + 1) * HS)
            kept[:, columns] = array[:, lanes(2 * n + parity)]
            sent[: array.shape[0], columns] = array[:, lanes(2 * n + 1 - parity)]
    if len(refs) == 5:
        sent[array.shape[0] :, :] = jnp.zeros((LINES, sent.shape[1]), jnp.bfloat16)
        sent[array.shape[0] :, :BLK] = refs[0][...]


def pair_body(mine, heard, whole):
    tokens = mine.shape[0]
    for parity, parts in enumerate(((mine, heard), (heard, mine))):

        @pl.when(position("tm")[1] == parity)
        def _():
            for n, part in enumerate(parts):
                whole[n * tokens : (n + 1) * tokens, :] = part[:tokens, :]


def pair_lines_body(lines, mine, heard, whole, rules, halo):
    tokens = mine.shape[0]
    pair_body(mine, heard, whole)
    theirs = heard[tokens:, :BLK]
    for parity, parts in enumerate(((lines[...], theirs), (theirs, lines[...]))):

        @pl.when(position("tm")[1] == parity)
        def _():
            for n, part in enumerate(parts):
                rules[n * LINES : (n + 1) * LINES, :] = part

    halo[: HALO * BLK, :] = whole[: HALO * BLK, :]
    halo[HALO * BLK :, :] = jnp.zeros((2 * LINES, halo.shape[1]), jnp.bfloat16)
    halo[HALO * BLK :, :BLK] = rules[...]


def of_head(ref, place, start, count):
    return ref[start : start + count, place * HS : (place + 1) * HS]


def window_of(pair, halo, place, part):
    tokens = QBD * BLK
    rows = [of_head(pair, place, part * tokens, (2 - part) * tokens)]
    rows.append(of_head(halo, place, 0, SPAN - (2 - part) * tokens))
    return jnp.concatenate(rows, axis=0)


def keys_of(pair, place, part):
    return of_head(pair, place, part * QBD * BLK, QBD * BLK)


def thirds(ref, first, last):
    part = ref[:, first * BLK : last * BLK]
    large, mass, dot = (part[i * KEPT : (i + 1) * KEPT] for i in range(3))
    return jnp.where(mass > 0, large, LOWEST), mass, dot


def merged(one, other):
    large = jnp.maximum(one[0], other[0])
    factors = [jnp.exp(part[0] - large) for part in (one, other)]
    return large, *(one[i] * factors[0] + other[i] * factors[1] for i in (1, 2))


def in_row(*parts):
    return tuple(jnp.concatenate(pieces, axis=1) for pieces in zip(*parts))


def stats_body(query, key, rules, halo, own, up, down, bias, partial):
    tables = [rules_of(rules[n * LINES : (n + 1) * LINES, :]) for n in range(2)]
    later = halo[HALO * BLK :, :BLK]
    tables += [rules_of(later[n * LINES : (n + 1) * LINES, :]) for n in range(2)]
    for part in range(2):
        fill_bias(tables[part : part + 3], bias.at[part])
        for place in range(KEPT):
            scores = nt(keys_of(key, place, part), window_of(query, halo, place, part)) * SCALE + bias[part]
            products = nt(keys_of(key, KEPT + place, part), window_of(query, halo, KEPT + place, part))
            largest = jnp.maximum(jnp.max(scores, axis=0, keepdims=True), LOWEST)
            weights = jnp.exp(scores - largest)
            rows = (largest, jnp.sum(weights, axis=0, keepdims=True), jnp.sum(weights * products, axis=0, keepdims=True))
            for i, row in enumerate(rows):
                partial[part, i * KEPT + place : i * KEPT + place + 1, :] = row
    first, second = partial.at[0], partial.at[1]
    whole = in_row(
        thirds(first, 0, QBD),
        merged(thirds(first, QBD, SLOTS), thirds(second, 0, SLOTS - QBD)),
        thirds(second, SLOTS - QBD, SLOTS),
    )
    for i, piece in enumerate(whole):
        own[i * KEPT : (i + 1) * KEPT, :] = piece
    up[...] = own[:, 2 * QBD * BLK :]
    down[...] = own[:, : HALO * BLK]


def totals_of(own, up, down):
    middle = 2 * QBD
    large, mass, dot = in_row(
        merged(thirds(own, 0, HALO), thirds(up, 0, HALO)),
        thirds(own, HALO, middle),
        merged(thirds(own, middle, middle + HALO), thirds(down, 0, HALO)),
    )
    inverse = jnp.where(mass > 0, 1.0 / jnp.where(mass > 0, mass, 1.0), 0.0)
    return large, inverse, dot * inverse


def line_of(total, index, place, part):
    start = part * QBD * BLK
    return total[index * KEPT + place : index * KEPT + place + 1, start : start + SPAN]


def terms_of(query, key, halo, bias, total, place, part):
    rows = window_of(query, halo, place, part)
    cotangent = window_of(query, halo, KEPT + place, part)
    scores = nt(keys_of(key, place, part), rows) * SCALE + bias[part]
    probs = jnp.exp(scores - line_of(total, 0, place, part)) * line_of(total, 1, place, part)
    products = nt(keys_of(key, KEPT + place, part), cotangent)
    return rows, cotangent, probs, (probs * (products - line_of(total, 2, place, part))).astype(jnp.bfloat16)


def lows_body(query, key, halo, bias, own, up, down, mine, other, sent, total):
    for index, value in enumerate(totals_of(own, up, down)):
        total[index * KEPT : (index + 1) * KEPT] = value
    keeps_key = position("fsdp")[1] == 0
    for place in range(KEPT):
        for part in range(2):
            rows, cotangent, probs, grad_scores = terms_of(query, key, halo, bias, total, place, part)
            value_grads = nn(probs.astype(jnp.bfloat16), cotangent)
            key_grads = nn(grad_scores, rows) * SCALE
            where = (slice(part * QBD * BLK, (part + 1) * QBD * BLK), slice(place * HS, (place + 1) * HS))
            mine[where] = jnp.where(keeps_key, key_grads, value_grads).astype(jnp.bfloat16)
            other[where] = jnp.where(keeps_key, value_grads, key_grads).astype(jnp.bfloat16)
    tokens = sent.shape[0]
    theirs = pl.ds(pl.multiple_of((1 - position("tm")[1]) * tokens, tokens), tokens)
    sent[:, :WIDE] = mine[theirs, :]
    sent[:, WIDE:] = other[theirs, :]


def queries_body(query, key, halo, bias, total, own, up):
    middle = 2 * QBD * BLK
    for place in range(KEPT):
        columns = slice(place * HS, (place + 1) * HS)
        terms = []
        for part in range(2):
            grad_scores = terms_of(query, key, halo, bias, total, place, part)[3]
            terms.append(tn(grad_scores, keys_of(key, place, part)) * SCALE)
        shift = QBD * BLK
        own[:shift, columns] = terms[0][:shift]
        own[shift:, columns] = terms[0][shift:middle] + terms[1][: middle - shift]
        up[: SPAN - middle, columns] = (terms[0][middle:] + terms[1][middle - shift : SPAN - shift]).astype(jnp.bfloat16)
        up[SPAN - middle :, columns] = terms[1][SPAN - shift :].astype(jnp.bfloat16)


def queries_sum_body(own, heard, kept, sent):
    tokens = kept.shape[0]
    parity = position("tm")[1]
    start = HALO * BLK
    for part in range(2):
        for out, side in ((kept, parity), (sent, 1 - parity)):

            @pl.when(side == part)
            def _():
                first, last = part * tokens, min((part + 1) * tokens, start)
                count = last - first
                total = own[first:last, :] + heard[first:last, :].astype(jnp.float32)
                out[:count, :] = total.astype(jnp.bfloat16)
                if count < tokens:
                    out[count:, :] = own[last : first + tokens, :].astype(jnp.bfloat16)


def queries_place_body(kept, heard, out, token):
    parity = position("tm")[1]
    for place, n in enumerate(ORDER):
        out[:, lanes(2 * n + parity)] = head_of(kept, place)
        out[:, lanes(2 * n + 1 - parity)] = head_of(heard, place)
    token[...] = jnp.zeros_like(token)


def head_of(ref, place):
    return ref[:, place * HS : (place + 1) * HS]


def turned_back(value, away, count):
    return lax.rem(value + (count - away), count)


def looked_up(table):
    shard = lax.axis_index("tm")
    entry = jnp.int32(table[0])
    for index, value in enumerate(table):
        entry = jnp.where(shard == index, jnp.int32(value), entry)
    return entry


def cut_body(width, x, *outs):
    for away, out in enumerate(outs):
        place = turned_back(position("fsdp")[0], away, len(outs))
        first = pl.multiple_of(place * width, width)
        out[...] = x[:, pl.ds(first, width)].T


def beside_body(*refs):
    out, start = refs[-1], 0
    for ref in refs[:-1]:
        out[:, start : start + ref.shape[1]] = ref[...]
        start += ref.shape[1]


def join_body(mine, heard, *outs):
    count, start = mine.shape[0], 0
    for out in outs:
        width = out.shape[1]
        for n, source in enumerate((mine, heard)):
            out[n * count : (n + 1) * count, :] = source[:, start : start + width]
        start += width


def weight_sum(turned, lows, tokens):
    chips = len(lows)
    parity = position("tm")[1]
    total = None
    for flip in range(2):
        for side in range(2):
            shard = parity if side == 0 else 1 - parity
            for away in range(chips):
                rows = pl.ds(pl.multiple_of(flip * 2 * tokens + shard * tokens, tokens), tokens)
                left = turned[2 * flip + side][:, away * tokens : (away + 1) * tokens]
                term = nn(left, lows[away][rows, :])
                total = term if total is None else total + term
    return total


def weight_body(tables, tokens, *refs):
    turned, lows, outs, total = refs[:4], refs[4 : -len(tables) - 1], refs[-len(tables) - 1 : -1], refs[-1]
    total[...] = weight_sum(turned, lows, tokens)
    for out, table in zip(outs, tables):
        out[...] = total[:, lanes(looked_up(table))].astype(out.dtype)


def plain_weight_body(tokens, *refs):
    refs[-1][...] = weight_sum(refs[:4], refs[4:-1], tokens)


def rows_body(mine, other, heard, *refs):
    weights, (out, token) = refs[:-2], refs[-2:]
    token[...] = jnp.zeros_like(token)
    tokens, width = out.shape[0], weights[0].shape[0]
    chips = len(weights) // 4
    chip, core = position("fsdp")
    parity = position("tm")[1]
    rows = pl.ds(pl.multiple_of(parity * tokens, tokens), tokens)
    first = jnp.where(core == 0, 1.0, 0.0).astype(jnp.bfloat16)
    second = jnp.where(core == 0, 0.0, 1.0).astype(jnp.bfloat16)
    own = (mine[rows, :], other[rows, :])
    theirs = (heard[:, :WIDE], heard[:, WIDE:])
    lows = [
        [pair[0] * a + pair[1] * b for pair in (own, theirs)] for a, b in ((first, second), (second, first))
    ]
    for away in range(chips):
        for flip in range(2):
            total = None
            for kind in range(2):
                weight = weights[4 * away + 2 * kind + flip]
                for low, side in zip(lows[kind], (parity, 1 - parity)):
                    factor = jnp.concatenate([weight[:, lanes(2 * m + side)] for m in ORDER], axis=1)
                    term = nt(low, factor)
                    total = term if total is None else total + term
            owner = 2 * lax.rem(chip + away, chips) + (core if flip == 0 else 1 - core)
            out[:, pl.ds(pl.multiple_of(owner * width, width), width)] = total.astype(out.dtype)


def choose_body(first, second, kept, sent):
    for core, (a, b) in enumerate(((first, second), (second, first))):

        @pl.when(position("fsdp")[1] == core)
        def _():
            kept[...] = a[...]
            sent[...] = b[...]


def grouped(refs, sizes):
    groups, start = [], 0
    for size in sizes:
        groups.append(refs[start : start + size])
        start += size
    return groups


def final_body(belongs, sizes, *refs):
    mine, send = refs[-2:]
    height = mine.shape[0]
    core = position("fsdp")[1]
    for n, parts in enumerate(grouped(refs[:-2], sizes)):

        @pl.when(looked_up(belongs) == n)
        def _():
            for out, side in ((mine, core), (send, 1 - core)):
                rows = pl.ds(pl.multiple_of(side * height, height), height)
                total = None
                for part in parts:
                    term = part[rows, :].astype(jnp.float32)
                    total = term if total is None else total + term
                out[...] = total


def shards(
    inputs, query_rows, saved_key_rows, value_rows, grad_out, key_weight, value_weight, block_pairs, pair_counts
):
    tokens = query_rows.shape[1]
    n_tm, n_fsdp = lax.axis_size("tm"), lax.axis_size("fsdp")
    shard = lax.axis_index("tm")
    d_model = inputs.shape[2]
    rows = d_model // n_fsdp
    half, chips = n_tm // 2, n_fsdp // 2
    q, k, v, g = query_rows[0], saved_key_rows[0], value_rows[0], grad_out[0]
    bf16, f32 = jnp.bfloat16, jnp.float32
    token = shape((8, HS), f32)

    def exchanged(array):
        return lax.ppermute(array, "fsdp", rolled_pairs(n_fsdp, 0, 1))

    def swapped(array):
        return lax.ppermute(array, "tm", rolled_pairs(n_tm, 0, 1))

    def fetched(array, away):
        return lax.ppermute(array, "fsdp", rolled_pairs(n_fsdp, away, 0))

    key_weights = [key_weight, *(fetched(key_weight, away) for away in range(1, chips))]
    value_weights = [value_weight, *(fetched(value_weight, away) for away in range(1, chips))]
    key_parts, value_parts = ([(array, exchanged(array)) for array in arrays] for arrays in (key_weights, value_weights))
    cuts = kernel_call(
        functools.partial(cut_body, 2 * rows), [shape((2 * rows, tokens), bf16)] * chips, (inputs[0],)
    )
    cuts = [fetched(piece, away) if away else piece for away, piece in enumerate(cuts)]

    pairs = jnp.where(jnp.arange(MAXP)[:, None] < pair_counts[0], block_pairs[0] - shard * QBD, UNUSED)
    lines = jnp.broadcast_to(pairs.T.reshape(LINES, 1), (LINES, BLK)).astype(bf16)
    query_kept, query_sent = kernel_call(
        split_body, [shape((tokens, 2 * WIDE), bf16), shape((tokens + LINES, 2 * WIDE), bf16)], (lines, q, g)
    )
    query_heard = swapped(query_sent)
    key_kept, key_sent = kernel_call(
        split_body, [shape((tokens, 2 * WIDE), bf16)] * 2, (k, v), after=(query_heard, *key_weights[1:])
    )
    key_heard = swapped(key_sent)
    query, rules, halo_sent = kernel_call(
        pair_lines_body,
        [
            shape((2 * tokens, 2 * WIDE), bf16),
            shape((2 * LINES, BLK), bf16),
            shape((HALO * BLK + 2 * LINES, 2 * WIDE), bf16),
        ],
        (lines, query_kept, query_heard),
    )
    halo = shifted(halo_sent, "tm", -2)

    (turned,) = kernel_call(
        beside_body, [shape((2 * rows, chips * tokens), bf16)], cuts, after=(key_heard,)
    )
    turned_pair = swapped(turned)
    (key,) = kernel_call(pair_body, [shape((2 * tokens, 2 * WIDE), bf16)], (key_kept, key_heard))

    own, up, down, bias = kernel_call(
        stats_body,
        [shape((3 * KEPT, count), f32) for count in (WINDOW, HALO * BLK, HALO * BLK)]
        + [shape((2, tokens, SPAN), f32)],
        (query, key, rules, halo),
        scratch=[pltpu.VMEM((2, 3 * KEPT, SPAN), f32)],
        flops=STATS_FLOPS,
    )
    up, down = shifted(up, "tm", 2), shifted(down, "tm", -2)
    mine, other, sent, total = kernel_call(
        lows_body,
        [shape((2 * tokens, WIDE), bf16)] * 2 + [shape((tokens, 2 * WIDE), bf16), shape((3 * KEPT, WINDOW), f32)],
        (query, key, halo, bias, own, up, down),
        after=(*(parts[1] for parts in key_parts), value_parts[0][1]),
    )
    widths = [len(members) * HS for members in SETS]
    lows = kernel_call(
        join_body,
        [shape((4 * tokens, width), bf16) for width in widths],
        (mine, exchanged(other)),
        after=(turned_pair, *value_weights[1:]),
    )
    groups = [[low, *(fetched(low, away) for away in range(1, chips))] for low in lows]
    query_kept, query_sent = kernel_call(
        split_body, [shape((tokens, 2 * WIDE), bf16), shape((tokens + LINES, 2 * WIDE), bf16)], (lines, q, g)
    )
    query_heard = swapped(query_sent)
    key_kept, key_sent = kernel_call(
        split_body, [shape((tokens, 2 * WIDE), bf16)] * 2, (k, v), after=(query_heard, *key_weights[1:])
    )
    key_heard = swapped(key_sent)
    query, rules, halo_sent = kernel_call(
        pair_lines_body,
        [
            shape((2 * tokens, 2 * WIDE), bf16),
            shape((2 * LINES, BLK), bf16),
            shape((HALO * BLK + 2 * LINES, 2 * WIDE), bf16),
        ],
        (lines, query_kept, query_heard),
    )
    halo = shifted(halo_sent, "tm", -2)

    (turned,) = kernel_call(
        beside_body, [shape((2 * rows, chips * tokens), bf16)], cuts, after=(key_heard,)
    )
    turned_pair = swapped(turned)
    (key,) = kernel_call(pair_body, [shape((2 * tokens, 2 * WIDE), bf16)], (key_kept, key_heard))

    own, up, down, bias = kernel_call(
        stats_body,
        [shape((3 * KEPT, count), f32) for count in (WINDOW, HALO * BLK, HALO * BLK)]
        + [shape((2, tokens, SPAN), f32)],
        (query, key, rules, halo),
        scratch=[pltpu.VMEM((2, 3 * KEPT, SPAN), f32)],
        flops=STATS_FLOPS,
    )
    up, down = shifted(up, "tm", 2), shifted(down, "tm", -2)
    mine, other, sent, total = kernel_call(
        lows_body,
        [shape((2 * tokens, WIDE), bf16)] * 2 + [shape((tokens, 2 * WIDE), bf16), shape((3 * KEPT, WINDOW), f32)],
        (query, key, halo, bias, own, up, down),
        after=(*(parts[1] for parts in key_parts), value_parts[0][1]),
    )
    widths = [len(members) * HS for members in SETS]
    lows = kernel_call(
        join_body,
        [shape((4 * tokens, width), bf16) for width in widths],
        (mine, exchanged(other)),
        after=(turned_pair, *value_weights[1:]),
    )
    groups = [[low, *(fetched(low, away) for away in range(1, chips))] for low in lows]
    query_own, query_up = kernel_call(
        queries_body,
        [shape((2 * tokens, WIDE), f32), shape((HALO * BLK, WIDE), bf16)],
        (query, key, halo, bias, total),
        after=lows,
    )
    query_kept, query_sent = kernel_call(
        queries_sum_body, [shape((tokens, WIDE), bf16)] * 2, (query_own, shifted(query_up, "tm", 2))
    )
    grad_query, query_token = kernel_call(
        queries_place_body, [shape((tokens, HD), bf16), token], (query_kept, swapped(query_sent))
    )

    result, result_token = kernel_call(
        rows_body,
        [shape((tokens, d_model), bf16), token],
        (
            mine,
            other,
            swapped(sent),
            *(part for pair in zip(key_parts, value_parts) for parts in pair for part in parts),
        ),
    )

    aligned = HD // n_tm == HS
    sides = (turned, turned_pair, exchanged(turned), exchanged(held(turned_pair, *lows)))
    sums, partials = [], []
    for index, (members, group, width) in enumerate(zip(SETS, groups, widths)):
        if not aligned:
            partials += kernel_call(
                functools.partial(plain_weight_body, tokens), [shape((2 * rows, width), f32)], (*sides, *group)
            )
            continue
        tables = []
        for away in range(half):
            tables.append([0] * n_tm)
            for y in range(2):
                for n, z in enumerate(members):
                    tables[-1][((z + away) % half) * 2 + y] = n
        chunks = kernel_call(
            functools.partial(weight_body, tables, tokens),
            [shape((2 * rows, HS), f32 if away == 0 else bf16) for away in range(half)],
            (*sides, *group),
            after=(partials[0], result_token) if index else (query_up,),
            scratch=[pltpu.VMEM((2 * rows, width), f32)],
            flops=1 if index else WEIGHT_FLOPS,
        )
        parcels = [chunks[0]]
        for away in range(1, half):
            routes = [(((z + away) % half) * 2 + y, z * 2 + y) for y in range(2) for z in members]
            parcels.append(lax.ppermute(chunks[away], "tm", routes))
        partials.append(chunks[0])
        sums.append(parcels)

    if aligned:
        belongs = [[j // 2 in members for members in SETS].index(True) for j in range(n_tm)]
        ours, theirs = kernel_call(
            functools.partial(final_body, belongs, [len(parcels) for parcels in sums]),
            [shape((rows, HS), f32)] * 2,
            [parcel for parcels in sums for parcel in parcels],
        )
    else:
        partial = jnp.concatenate(partials, axis=1)
        heads = [partial[:, ORDER.index(n) * HS : (ORDER.index(n) + 1) * HS] for n in range(KEPT)]
        parity, core = shard % 2, lax.axis_index("fsdp") % 2
        spread = [jnp.where(parity == y, heads[n], 0.0) for n in range(KEPT) for y in range(2)]
        whole = lax.psum_scatter(jnp.concatenate(spread, axis=1), "tm", scatter_dimension=1, tiled=True)
        ours, theirs = (lax.dynamic_slice_in_dim(whole, side * rows, rows, 0) for side in (core, 1 - core))
    key_total, value_total = kernel_call(
        choose_body, [shape(ours.shape, f32)] * 2, (ours, exchanged(theirs))
    )
    return (grad_query[None], result[None], key_total, value_total)


def solution(mesh):
    return jax.shard_map(
        shards,
        mesh=mesh,
        in_specs=(
            P("fsdp", "tm", None),
            P("fsdp", "tm", None),
            P("fsdp", "tm", None),
            P("fsdp", "tm", None),
            P("fsdp", "tm", None),
            P("fsdp", None),
            P("fsdp", None),
            P("tm", None, None),
            P("tm"),
        ),
        out_specs=(P("fsdp", "tm", None), P("fsdp", "tm", None), P("fsdp", "tm"), P("fsdp", "tm")),
        check_vma=False,
    )
```

```python
import functools

import jax
import jax.numpy as jnp
from jax import lax
from jax.experimental import pallas as pl
from jax.experimental.pallas import tpu as pltpu
from jax.sharding import PartitionSpec as P

H = 8
HS = 128
BLK = 128
HD = 1024
QBD = 2
REACH = 2
MAXP = 8
WB = 4
SLOTS = QBD + WB - 1
UNUSED = 100
STATS_FLOPS = 20_000_000_000
WEIGHT_FLOPS = 1
VMEM_LIMIT = 16 * 1024 * 1024
SPAN = SLOTS * BLK
LOWEST = -1e29
MASKED = -1e30
SCALE = HS ** (-0.5)
SETS = ((0, 3), (1, 2))
ORDER = tuple(n for members in SETS for n in members)
KEPT = len(ORDER)
WIDE = KEPT * HS
HALO = WB - 1
WINDOW = (2 * QBD + HALO) * BLK
LINES = 2 * MAXP
VMEM = pl.BlockSpec(memory_space=pltpu.VMEM)
ANY = pl.BlockSpec(memory_space=pl.ANY)


def kernel_call(body, outs, operands, after=(), scratch=(), flops=1):
    count = len(operands)

    def run(*refs):
        body(*refs[:count], *refs[count + len(after) :])

    return pl.pallas_call(
        run,
        out_shape=tuple(outs),
        in_specs=[VMEM] * count + [ANY] * len(after),
        out_specs=tuple([VMEM] * len(outs)),
        scratch_shapes=list(scratch),
        compiler_params=pltpu.CompilerParams(vmem_limit_bytes=VMEM_LIMIT),
        cost_estimate=pl.CostEstimate(flops=flops, bytes_accessed=1, transcendentals=0),
    )(*operands, *after)


def copy_body(value, out):
    out[...] = value[...]


def held(value, *others):
    (copy,) = kernel_call(copy_body, [shape(value.shape, value.dtype)], (value,), after=others)
    return copy


def shape(dims, kind):
    return jax.ShapeDtypeStruct(dims, kind)


def shifted(value, axis, steps):
    count = lax.axis_size(axis)
    return lax.ppermute(
        value, axis, [(s, s + steps) for s in range(max(0, -steps), min(count, count - steps))]
    )


def rolled_pairs(count, far, flip):
    half = count // 2
    return [(((a + far) % half) * 2 + (b ^ flip), a * 2 + b) for a in range(half) for b in range(2)]


def nt(left, right):
    return lax.dot_general(left, right, (((1,), (1,)), ((), ())), preferred_element_type=jnp.float32)


def tn(left, right):
    return lax.dot_general(left, right, (((0,), (0,)), ((), ())), preferred_element_type=jnp.float32)


def nn(left, right):
    return jnp.dot(left, right, preferred_element_type=jnp.float32)


def rules_of(lines):
    lines = lines.astype(jnp.float32)
    queries, keys = lines[:MAXP], lines[MAXP:]
    found = {}
    for query in range(QBD):
        for back in range(WB):
            hit = jnp.where((queries == query) & (keys == query - back), 0.0, MASKED)
            found[query, back] = jnp.max(hit, axis=0, keepdims=True)
    return found


def fill_bias(sets, bias):
    rows = lax.broadcasted_iota(jnp.int32, (BLK, BLK), 0)
    columns = lax.broadcasted_iota(jnp.int32, (BLK, BLK), 1)
    for key in range(QBD):
        for slot in range(SLOTS):
            place = (pl.ds(key * BLK, BLK), pl.ds(slot * BLK, BLK))
            back = slot - key
            if not 0 <= back < WB:
                bias[place] = jnp.full((BLK, BLK), MASKED, jnp.float32)
                continue
            block = jnp.broadcast_to(sets[slot // QBD][slot % QBD, back], (BLK, BLK))
            if slot == key:
                block = jnp.where(rows <= columns, block, MASKED)
            bias[place] = block


def position(axis):
    index = lax.axis_index(axis)
    return index // 2, index % 2


def lanes(index):
    return pl.ds(pl.multiple_of(index * HS, HS), HS)


def split_body(*refs):
    first, second = refs[-4:-2]
    kept, sent = refs[-2:]
    parity = position("tm")[1]
    for side, array in enumerate((first, second)):
        for place, n in enumerate(ORDER):
            columns = slice((side * KEPT + place) * HS, (side * KEPT + place + 1) * HS)
            kept[:, columns] = array[:, lanes(2 * n + parity)]
            sent[: array.shape[0], columns] = array[:, lanes(2 * n + 1 - parity)]
    if len(refs) == 5:
        sent[array.shape[0] :, :] = jnp.zeros((LINES, sent.shape[1]), jnp.bfloat16)
        sent[array.shape[0] :, :BLK] = refs[0][...]


def pair_body(mine, heard, whole):
    tokens = mine.shape[0]
    for parity, parts in enumerate(((mine, heard), (heard, mine))):

        @pl.when(position("tm")[1] == parity)
        def _():
            for n, part in enumerate(parts):
                whole[n * tokens : (n + 1) * tokens, :] = part[:tokens, :]


def pair_lines_body(lines, mine, heard, whole, rules, halo):
    tokens = mine.shape[0]
    pair_body(mine, heard, whole)
    theirs = heard[tokens:, :BLK]
    for parity, parts in enumerate(((lines[...], theirs), (theirs, lines[...]))):

        @pl.when(position("tm")[1] == parity)
        def _():
            for n, part in enumerate(parts):
                rules[n * LINES : (n + 1) * LINES, :] = part

    halo[: HALO * BLK, :] = whole[: HALO * BLK, :]
    halo[HALO * BLK :, :] = jnp.zeros((2 * LINES, halo.shape[1]), jnp.bfloat16)
    halo[HALO * BLK :, :BLK] = rules[...]


def of_head(ref, place, start, count):
    return ref[start : start + count, place * HS : (place + 1) * HS]


def window_of(pair, halo, place, part):
    tokens = QBD * BLK
    rows = [of_head(pair, place, part * tokens, (2 - part) * tokens)]
    rows.append(of_head(halo, place, 0, SPAN - (2 - part) * tokens))
    return jnp.concatenate(rows, axis=0)


def keys_of(pair, place, part):
    return of_head(pair, place, part * QBD * BLK, QBD * BLK)


def thirds(ref, first, last):
    part = ref[:, first * BLK : last * BLK]
    large, mass, dot = (part[i * KEPT : (i + 1) * KEPT] for i in range(3))
    return jnp.where(mass > 0, large, LOWEST), mass, dot


def merged(one, other):
    large = jnp.maximum(one[0], other[0])
    factors = [jnp.exp(part[0] - large) for part in (one, other)]
    return large, *(one[i] * factors[0] + other[i] * factors[1] for i in (1, 2))


def in_row(*parts):
    return tuple(jnp.concatenate(pieces, axis=1) for pieces in zip(*parts))


def stats_body(query, key, rules, halo, own, up, down, bias, partial):
    tables = [rules_of(rules[n * LINES : (n + 1) * LINES, :]) for n in range(2)]
    later = halo[HALO * BLK :, :BLK]
    tables += [rules_of(later[n * LINES : (n + 1) * LINES, :]) for n in range(2)]
    for part in range(2):
        fill_bias(tables[part : part + 3], bias.at[part])
        for place in range(KEPT):
            scores = nt(keys_of(key, place, part), window_of(query, halo, place, part)) * SCALE + bias[part]
            products = nt(keys_of(key, KEPT + place, part), window_of(query, halo, KEPT + place, part))
            largest = jnp.maximum(jnp.max(scores, axis=0, keepdims=True), LOWEST)
            weights = jnp.exp(scores - largest)
            rows = (largest, jnp.sum(weights, axis=0, keepdims=True), jnp.sum(weights * products, axis=0, keepdims=True))
            for i, row in enumerate(rows):
                partial[part, i * KEPT + place : i * KEPT + place + 1, :] = row
    first, second = partial.at[0], partial.at[1]
    whole = in_row(
        thirds(first, 0, QBD),
        merged(thirds(first, QBD, SLOTS), thirds(second, 0, SLOTS - QBD)),
        thirds(second, SLOTS - QBD, SLOTS),
    )
    for i, piece in enumerate(whole):
        own[i * KEPT : (i + 1) * KEPT, :] = piece
    up[...] = own[:, 2 * QBD * BLK :]
    down[...] = own[:, : HALO * BLK]


def totals_of(own, up, down):
    middle = 2 * QBD
    large, mass, dot = in_row(
        merged(thirds(own, 0, HALO), thirds(up, 0, HALO)),
        thirds(own, HALO, middle),
        merged(thirds(own, middle, middle + HALO), thirds(down, 0, HALO)),
    )
    inverse = jnp.where(mass > 0, 1.0 / jnp.where(mass > 0, mass, 1.0), 0.0)
    return large, inverse, dot * inverse


def line_of(total, index, place, part):
    start = part * QBD * BLK
    return total[index * KEPT + place : index * KEPT + place + 1, start : start + SPAN]


def terms_of(query, key, halo, bias, total, place, part):
    rows = window_of(query, halo, place, part)
    cotangent = window_of(query, halo, KEPT + place, part)
    scores = nt(keys_of(key, place, part), rows) * SCALE + bias[part]
    probs = jnp.exp(scores - line_of(total, 0, place, part)) * line_of(total, 1, place, part)
    products = nt(keys_of(key, KEPT + place, part), cotangent)
    return rows, cotangent, probs, (probs * (products - line_of(total, 2, place, part))).astype(jnp.bfloat16)


def lows_body(query, key, halo, bias, own, up, down, mine, other, sent, total):
    for index, value in enumerate(totals_of(own, up, down)):
        total[index * KEPT : (index + 1) * KEPT] = value
    keeps_key = position("fsdp")[1] == 0
    for place in range(KEPT):
        for part in range(2):
            rows, cotangent, probs, grad_scores = terms_of(query, key, halo, bias, total, place, part)
            value_grads = nn(probs.astype(jnp.bfloat16), cotangent)
            key_grads = nn(grad_scores, rows) * SCALE
            where = (slice(part * QBD * BLK, (part + 1) * QBD * BLK), slice(place * HS, (place + 1) * HS))
            mine[where] = jnp.where(keeps_key, key_grads, value_grads).astype(jnp.bfloat16)
            other[where] = jnp.where(keeps_key, value_grads, key_grads).astype(jnp.bfloat16)
    tokens = sent.shape[0]
    theirs = pl.ds(pl.multiple_of((1 - position("tm")[1]) * tokens, tokens), tokens)
    sent[:, :WIDE] = mine[theirs, :]
    sent[:, WIDE:] = other[theirs, :]


def queries_body(query, key, halo, bias, total, own, up):
    middle = 2 * QBD * BLK
    for place in range(KEPT):
        columns = slice(place * HS, (place + 1) * HS)
        terms = []
        for part in range(2):
            grad_scores = terms_of(query, key, halo, bias, total, place, part)[3]
            terms.append(tn(grad_scores, keys_of(key, place, part)) * SCALE)
        shift = QBD * BLK
        own[:shift, columns] = terms[0][:shift]
        own[shift:, columns] = terms[0][shift:middle] + terms[1][: middle - shift]
        up[: SPAN - middle, columns] = (terms[0][middle:] + terms[1][middle - shift : SPAN - shift]).astype(jnp.bfloat16)
        up[SPAN - middle :, columns] = terms[1][SPAN - shift :].astype(jnp.bfloat16)


def queries_sum_body(own, heard, kept, sent):
    tokens = kept.shape[0]
    parity = position("tm")[1]
    start = HALO * BLK
    for part in range(2):
        for out, side in ((kept, parity), (sent, 1 - parity)):

            @pl.when(side == part)
            def _():
                first, last = part * tokens, min((part + 1) * tokens, start)
                count = last - first
                total = own[first:last, :] + heard[first:last, :].astype(jnp.float32)
                out[:count, :] = total.astype(jnp.bfloat16)
                if count < tokens:
                    out[count:, :] = own[last : first + tokens, :].astype(jnp.bfloat16)


def queries_place_body(kept, heard, out, token):
    parity = position("tm")[1]
    for place, n in enumerate(ORDER):
        out[:, lanes(2 * n + parity)] = head_of(kept, place)
        out[:, lanes(2 * n + 1 - parity)] = head_of(heard, place)
    token[...] = jnp.zeros_like(token)


def head_of(ref, place):
    return ref[:, place * HS : (place + 1) * HS]


def turned_back(value, away, count):
    return lax.rem(value + (count - away), count)


def looked_up(table):
    shard = lax.axis_index("tm")
    entry = jnp.int32(table[0])
    for index, value in enumerate(table):
        entry = jnp.where(shard == index, jnp.int32(value), entry)
    return entry


def cut_body(width, x, *outs):
    for away, out in enumerate(outs):
        place = turned_back(position("fsdp")[0], away, len(outs))
        first = pl.multiple_of(place * width, width)
        out[...] = x[:, pl.ds(first, width)].T


def beside_body(*refs):
    out, start = refs[-1], 0
    for ref in refs[:-1]:
        out[:, start : start + ref.shape[1]] = ref[...]
        start += ref.shape[1]


def join_body(mine, heard, *outs):
    count, start = mine.shape[0], 0
    for out in outs:
        width = out.shape[1]
        for n, source in enumerate((mine, heard)):
            out[n * count : (n + 1) * count, :] = source[:, start : start + width]
        start += width


def weight_sum(turned, lows, tokens):
    chips = len(lows)
    parity = position("tm")[1]
    total = None
    for flip in range(2):
        for side in range(2):
            shard = parity if side == 0 else 1 - parity
            for away in range(chips):
                rows = pl.ds(pl.multiple_of(flip * 2 * tokens + shard * tokens, tokens), tokens)
                left = turned[2 * flip + side][:, away * tokens : (away + 1) * tokens]
                term = nn(left, lows[away][rows, :])
                total = term if total is None else total + term
    return total


def weight_body(tables, tokens, *refs):
    turned, lows, outs, total = refs[:4], refs[4 : -len(tables) - 1], refs[-len(tables) - 1 : -1], refs[-1]
    total[...] = weight_sum(turned, lows, tokens)
    for out, table in zip(outs, tables):
        out[...] = total[:, lanes(looked_up(table))].astype(out.dtype)


def plain_weight_body(tokens, *refs):
    refs[-1][...] = weight_sum(refs[:4], refs[4:-1], tokens)


def rows_body(mine, other, heard, *refs):
    weights, (out, token) = refs[:-2], refs[-2:]
    token[...] = jnp.zeros_like(token)
    tokens, width = out.shape[0], weights[0].shape[0]
    chips = len(weights) // 4
    chip, core = position("fsdp")
    parity = position("tm")[1]
    rows = pl.ds(pl.multiple_of(parity * tokens, tokens), tokens)
    first = jnp.where(core == 0, 1.0, 0.0).astype(jnp.bfloat16)
    second = jnp.where(core == 0, 0.0, 1.0).astype(jnp.bfloat16)
    own = (mine[rows, :], other[rows, :])
    theirs = (heard[:, :WIDE], heard[:, WIDE:])
    lows = [
        [pair[0] * a + pair[1] * b for pair in (own, theirs)] for a, b in ((first, second), (second, first))
    ]
    for away in range(chips):
        for flip in range(2):
            total = None
            for kind in range(2):
                weight = weights[4 * away + 2 * kind + flip]
                for low, side in zip(lows[kind], (parity, 1 - parity)):
                    factor = jnp.concatenate([weight[:, lanes(2 * m + side)] for m in ORDER], axis=1)
                    term = nt(low, factor)
                    total = term if total is None else total + term
            owner = 2 * lax.rem(chip + away, chips) + (core if flip == 0 else 1 - core)
            out[:, pl.ds(pl.multiple_of(owner * width, width), width)] = total.astype(out.dtype)


def choose_body(first, second, kept, sent):
    for core, (a, b) in enumerate(((first, second), (second, first))):

        @pl.when(position("fsdp")[1] == core)
        def _():
            kept[...] = a[...]
            sent[...] = b[...]


def grouped(refs, sizes):
    groups, start = [], 0
    for size in sizes:
        groups.append(refs[start : start + size])
        start += size
    return groups


def final_body(belongs, sizes, *refs):
    mine, send = refs[-2:]
    height = mine.shape[0]
    core = position("fsdp")[1]
    for n, parts in enumerate(grouped(refs[:-2], sizes)):

        @pl.when(looked_up(belongs) == n)
        def _():
            for out, side in ((mine, core), (send, 1 - core)):
                rows = pl.ds(pl.multiple_of(side * height, height), height)
                total = None
                for part in parts:
                    term = part[rows, :].astype(jnp.float32)
                    total = term if total is None else total + term
                out[...] = total


def shards(
    inputs, query_rows, saved_key_rows, value_rows, grad_out, key_weight, value_weight, block_pairs, pair_counts
):
    tokens = query_rows.shape[1]
    n_tm, n_fsdp = lax.axis_size("tm"), lax.axis_size("fsdp")
    shard = lax.axis_index("tm")
    d_model = inputs.shape[2]
    rows = d_model // n_fsdp
    half, chips = n_tm // 2, n_fsdp // 2
    q, k, v, g = query_rows[0], saved_key_rows[0], value_rows[0], grad_out[0]
    bf16, f32 = jnp.bfloat16, jnp.float32
    token = shape((8, HS), f32)

    def exchanged(array):
        return lax.ppermute(array, "fsdp", rolled_pairs(n_fsdp, 0, 1))

    def swapped(array):
        return lax.ppermute(array, "tm", rolled_pairs(n_tm, 0, 1))

    def fetched(array, away):
        return lax.ppermute(array, "fsdp", rolled_pairs(n_fsdp, away, 0))

    key_weights = [key_weight, *(fetched(key_weight, away) for away in range(1, chips))]
    value_weights = [value_weight, *(fetched(value_weight, away) for away in range(1, chips))]
    key_parts, value_parts = ([(array, exchanged(array)) for array in arrays] for arrays in (key_weights, value_weights))
    cuts = kernel_call(
        functools.partial(cut_body, 2 * rows), [shape((2 * rows, tokens), bf16)] * chips, (inputs[0],)
    )
    cuts = [fetched(piece, away) if away else piece for away, piece in enumerate(cuts)]

    pairs = jnp.where(jnp.arange(MAXP)[:, None] < pair_counts[0], block_pairs[0] - shard * QBD, UNUSED)
    lines = jnp.broadcast_to(pairs.T.reshape(LINES, 1), (LINES, BLK)).astype(bf16)
    query_kept, query_sent = kernel_call(
        split_body, [shape((tokens, 2 * WIDE), bf16), shape((tokens + LINES, 2 * WIDE), bf16)], (lines, q, g)
    )
    query_heard = swapped(query_sent)
    key_kept, key_sent = kernel_call(
        split_body, [shape((tokens, 2 * WIDE), bf16)] * 2, (k, v), after=(query_heard, *key_weights[1:])
    )
    key_heard = swapped(key_sent)
    query, rules, halo_sent = kernel_call(
        pair_lines_body,
        [
            shape((2 * tokens, 2 * WIDE), bf16),
            shape((2 * LINES, BLK), bf16),
            shape((HALO * BLK + 2 * LINES, 2 * WIDE), bf16),
        ],
        (lines, query_kept, query_heard),
    )
    halo = shifted(halo_sent, "tm", -2)

    (turned,) = kernel_call(
        beside_body, [shape((2 * rows, chips * tokens), bf16)], cuts, after=(key_heard,)
    )
    turned_pair = swapped(turned)
    (key,) = kernel_call(pair_body, [shape((2 * tokens, 2 * WIDE), bf16)], (key_kept, key_heard))

    own, up, down, bias = kernel_call(
        stats_body,
        [shape((3 * KEPT, count), f32) for count in (WINDOW, HALO * BLK, HALO * BLK)]
        + [shape((2, tokens, SPAN), f32)],
        (query, key, rules, halo),
        scratch=[pltpu.VMEM((2, 3 * KEPT, SPAN), f32)],
        flops=STATS_FLOPS,
    )
    up, down = shifted(up, "tm", 2), shifted(down, "tm", -2)
    mine, other, sent, total = kernel_call(
        lows_body,
        [shape((2 * tokens, WIDE), bf16)] * 2 + [shape((tokens, 2 * WIDE), bf16), shape((3 * KEPT, WINDOW), f32)],
        (query, key, halo, bias, own, up, down),
        after=(*(parts[1] for parts in key_parts), value_parts[0][1]),
    )
    widths = [len(members) * HS for members in SETS]
    lows = kernel_call(
        join_body,
        [shape((4 * tokens, width), bf16) for width in widths],
        (mine, exchanged(other)),
        after=(turned_pair,),
    )
    groups = [[low, *(fetched(low, away) for away in range(1, chips))] for low in lows]
    query_kept, query_sent = kernel_call(
        split_body, [shape((tokens, 2 * WIDE), bf16), shape((tokens + LINES, 2 * WIDE), bf16)], (lines, q, g)
    )
    query_heard = swapped(query_sent)
    key_kept, key_sent = kernel_call(
        split_body, [shape((tokens, 2 * WIDE), bf16)] * 2, (k, v), after=(query_heard, *key_weights[1:])
    )
    key_heard = swapped(key_sent)
    query, rules, halo_sent = kernel_call(
        pair_lines_body,
        [
            shape((2 * tokens, 2 * WIDE), bf16),
            shape((2 * LINES, BLK), bf16),
            shape((HALO * BLK + 2 * LINES, 2 * WIDE), bf16),
        ],
        (lines, query_kept, query_heard),
    )
    halo = shifted(halo_sent, "tm", -2)

    (turned,) = kernel_call(
        beside_body, [shape((2 * rows, chips * tokens), bf16)], cuts, after=(key_heard,)
    )
    turned_pair = swapped(turned)
    (key,) = kernel_call(pair_body, [shape((2 * tokens, 2 * WIDE), bf16)], (key_kept, key_heard))

    own, up, down, bias = kernel_call(
        stats_body,
        [shape((3 * KEPT, count), f32) for count in (WINDOW, HALO * BLK, HALO * BLK)]
        + [shape((2, tokens, SPAN), f32)],
        (query, key, rules, halo),
        scratch=[pltpu.VMEM((2, 3 * KEPT, SPAN), f32)],
        flops=STATS_FLOPS,
    )
    up, down = shifted(up, "tm", 2), shifted(down, "tm", -2)
    mine, other, sent, total = kernel_call(
        lows_body,
        [shape((2 * tokens, WIDE), bf16)] * 2 + [shape((tokens, 2 * WIDE), bf16), shape((3 * KEPT, WINDOW), f32)],
        (query, key, halo, bias, own, up, down),
        after=(*(parts[1] for parts in key_parts), value_parts[0][1]),
    )
    widths = [len(members) * HS for members in SETS]
    lows = kernel_call(
        join_body,
        [shape((4 * tokens, width), bf16) for width in widths],
        (mine, exchanged(other)),
        after=(turned_pair,),
    )
    groups = [[low, *(fetched(low, away) for away in range(1, chips))] for low in lows]
    query_own, query_up = kernel_call(
        queries_body,
        [shape((2 * tokens, WIDE), f32), shape((HALO * BLK, WIDE), bf16)],
        (query, key, halo, bias, total),
        after=lows,
    )
    query_kept, query_sent = kernel_call(
        queries_sum_body, [shape((tokens, WIDE), bf16)] * 2, (query_own, shifted(query_up, "tm", 2))
    )
    grad_query, query_token = kernel_call(
        queries_place_body, [shape((tokens, HD), bf16), token], (query_kept, swapped(query_sent))
    )

    result, result_token = kernel_call(
        rows_body,
        [shape((tokens, d_model), bf16), token],
        (
            mine,
            other,
            swapped(sent),
            *(part for pair in zip(key_parts, value_parts) for parts in pair for part in parts),
        ),
    )

    aligned = HD // n_tm == HS
    sides = (turned, turned_pair, exchanged(turned), exchanged(held(turned_pair, *lows)))
    sums, partials = [], []
    for index, (members, group, width) in enumerate(zip(SETS, groups, widths)):
        if not aligned:
            partials += kernel_call(
                functools.partial(plain_weight_body, tokens), [shape((2 * rows, width), f32)], (*sides, *group)
            )
            continue
        tables = []
        for away in range(half):
            tables.append([0] * n_tm)
            for y in range(2):
                for n, z in enumerate(members):
                    tables[-1][((z + away) % half) * 2 + y] = n
        chunks = kernel_call(
            functools.partial(weight_body, tables, tokens),
            [shape((2 * rows, HS), f32 if away == 0 else bf16) for away in range(half)],
            (*sides, *group),
            after=(partials[0],) if index else (query_up,),
            scratch=[pltpu.VMEM((2 * rows, width), f32)],
            flops=1 if index else WEIGHT_FLOPS,
        )
        parcels = [chunks[0]]
        for away in range(1, half):
            routes = [(((z + away) % half) * 2 + y, z * 2 + y) for y in range(2) for z in members]
            parcels.append(lax.ppermute(chunks[away], "tm", routes))
        partials.append(chunks[0])
        sums.append(parcels)

    if aligned:
        belongs = [[j // 2 in members for members in SETS].index(True) for j in range(n_tm)]
        ours, theirs = kernel_call(
            functools.partial(final_body, belongs, [len(parcels) for parcels in sums]),
            [shape((rows, HS), f32)] * 2,
            [parcel for parcels in sums for parcel in parcels],
            after=(result_token,),
        )
    else:
        partial = jnp.concatenate(partials, axis=1)
        heads = [partial[:, ORDER.index(n) * HS : (ORDER.index(n) + 1) * HS] for n in range(KEPT)]
        parity, core = shard % 2, lax.axis_index("fsdp") % 2
        spread = [jnp.where(parity == y, heads[n], 0.0) for n in range(KEPT) for y in range(2)]
        whole = lax.psum_scatter(jnp.concatenate(spread, axis=1), "tm", scatter_dimension=1, tiled=True)
        ours, theirs = (lax.dynamic_slice_in_dim(whole, side * rows, rows, 0) for side in (core, 1 - core))
    key_total, value_total = kernel_call(
        choose_body, [shape(ours.shape, f32)] * 2, (ours, exchanged(theirs))
    )
    return (grad_query[None], result[None], key_total, value_total)


def solution(mesh):
    return jax.shard_map(
        shards,
        mesh=mesh,
        in_specs=(
            P("fsdp", "tm", None),
            P("fsdp", "tm", None),
            P("fsdp", "tm", None),
            P("fsdp", "tm", None),
            P("fsdp", "tm", None),
            P("fsdp", None),
            P("fsdp", None),
            P("tm", None, None),
            P("tm"),
        ),
        out_specs=(P("fsdp", "tm", None), P("fsdp", "tm", None), P("fsdp", "tm"), P("fsdp", "tm")),
        check_vma=False,
    )
```
